256 devices in a mesh: seq: 16 (over z, core), mp: 4 (over x), batch: 4 (over y).
Axes of the slice: x: 4, y: 4, z: 8, core: 2. Of those that a mesh axis runs over, the one named last changes fastest.
Arguments:
- latent: bfloat16 [32768, 2048], P(('batch', 'seq')), parts along dimension 0, may hold values from -6 to 6
- order: int32 [8192], P('seq'), may hold values from 0 to 8191, as said below
- inverse: int32 [8192], P('seq'), may hold values from 0 to 8191
- w_gate: bfloat16 [2048, 4096], P(None, 'mp'), may hold values from -0.125 to 0.125
- w_value: bfloat16 [2048, 4096], P(None, 'mp'), may hold values from -0.125 to 0.125
- w_input_output: bfloat16 [2048, 256], replicated, may hold values from -0.125 to 0.125
- w_step: bfloat16 [2048, 32], P(None, 'mp'), may hold values from -0.125 to 0.125
- conv_value: float32 [4, 4096], P(None, 'mp'), may hold values from -3 to 3
- conv_input_output: float32 [4, 256], replicated, may hold values from -3 to 3
- step_bias: float32 [32], P('mp'), may hold values from -4.5 to -2
- log_rate: float32 [32], P('mp'), may hold values from -8 to 1
- skip_gain: float32 [32], P('mp'), may hold values from 0.5 to 1.5
- norm_gain: float32 [4096], P('mp'), may hold values from 0.5 to 1.5
Outputs:
- mixed_out: bfloat16 [32768, 4096], P(('batch', 'seq'), 'mp'), parts along dimension 0
The draws below stay inside these ranges and needn't reach their ends.
There are 4 independent parts, one for each index of `batch`. The reference program is written for one: setup_inputs(seed, part) draws one part's arguments, and reference() takes and returns one part's arrays. A program takes and returns all parts, laid end to end along the dimension named above; an argument that names none is the same for every part. Nothing has to cross between parts.
Inputs may be any that keep to these rules, and one draw needn't show every extreme that they name: order and inverse are permutations of 0 to 8191 and inverse of each other. Of the 512 storage rows of one index of seq, at most 64 have their scan positions on one index of seq, and the same holds for scan positions and storage rows; in every draw some pair of indices reaches 64.
All inputs are finite; a program needn't handle non-finite values.
Results may differ from the reference program's by a relative error of at most 0.012.
Values may be sent and summed in bfloat16 or wider, within the bound.
No kernel may reach another device: no remote copies, remote signals or barrier semaphores. Data moves between devices by JAX's collectives and lax.ppermute only.
A program may use at most 128 MiB of HBM per device.

```python
import jax
import jax.numpy as jnp
from jax import lax

D = 2048
DI = 4096
H = 32
N = 128
K = 4
Q = 128
TOK_DEV = 512
HEAD = 128
LENGTH = 8192


def shuffled(sub_key):
    return jax.random.permutation(sub_key, TOK_DEV)


def scan_order(key):
    devices = LENGTH // TOK_DEV
    piece_rows = TOK_DEV // devices
    key_off, key_label, key_src, key_dst = jax.random.split(key, 4)
    offsets = jax.random.permutation(key_off, devices).astype(jnp.int32)
    offsets = offsets.at[devices - 1].set(offsets[0])
    labels = jax.random.permutation(key_label, devices).astype(jnp.int32)
    src_order = jax.vmap(shuffled)(jax.random.split(key_src, devices)).astype(jnp.int32)
    dst_order = jax.vmap(shuffled)(jax.random.split(key_dst, devices)).astype(jnp.int32)
    source = jnp.arange(devices, dtype=jnp.int32)[:, None, None]
    pieces = jnp.arange(devices, dtype=jnp.int32)[None, :, None]
    within = jnp.arange(piece_rows, dtype=jnp.int32)[None, None, :]
    slot_index = pieces * piece_rows + within
    dest_dev = (labels[:, None, None] + offsets[None, :, None]) % devices
    src_rows = source * TOK_DEV + src_order[source, slot_index]
    tgt_rows = dest_dev * TOK_DEV + dst_order[dest_dev, slot_index]
    src_flat = jnp.broadcast_to(src_rows, (devices, devices, piece_rows)).reshape(-1)
    tgt_flat = jnp.broadcast_to(tgt_rows, (devices, devices, piece_rows)).reshape(-1)
    inverse_rows = jnp.zeros((LENGTH,), jnp.int32).at[src_flat].set(tgt_flat)
    forward_rows = jnp.zeros((LENGTH,), jnp.int32).at[tgt_flat].set(src_flat)
    return (forward_rows, inverse_rows)


def draw_order(key, part):
    return scan_order(key)[0]


def draw_inverse(key, part):
    return scan_order(key)[1]


def draw_log_rate(key, part):
    key = jax.random.fold_in(key, 7)
    return jax.random.uniform(key, (H,), jnp.float32, -7.0, 1.0)


def shard_levels(stream_key, shape, cuts, smallest, top_value):
    loudness, own = 1.0, jax.random.fold_in(stream_key, 6)
    for position, parts in cuts:
        draws = jnp.exp(jax.random.uniform(jax.random.fold_in(own, position), (parts,), jnp.float32, smallest / len(cuts), top_value / len(cuts)))
        loudness = loudness * jnp.repeat(draws, shape[position] // parts).reshape([-1 if axis == position else 1 for axis in range(len(shape))])
    return loudness


def normal_values(key, extent, width, reach, cuts=(), held_as=jnp.bfloat16):
    loudness = shard_levels(key, extent, cuts, -0.22, 0.18) if cuts else 1.0
    drawn = jax.random.normal(key, extent, jnp.float32) * width * loudness
    return jnp.minimum(jnp.maximum(drawn, -reach), reach).astype(held_as)


def setup_inputs(seed: int = 0, part: int = 0) -> dict:
    key_of = jax.random.split(jax.random.key(seed), 14)
    own_keys = jax.random.split(jax.random.fold_in(key_of[13], part), 14)
    latent = normal_values(own_keys[0], (LENGTH, D), 1.0, 6.0, ((0, 16),))
    order = draw_order(jax.random.fold_in(key_of[13], 71), part)
    inverse = draw_inverse(jax.random.fold_in(key_of[13], 71), part)
    w_gate = normal_values(key_of[3], (D, DI), D ** -0.5, 0.125, ((1, 4),))
    w_value = normal_values(key_of[4], (D, DI), D ** -0.5, 0.125, ((1, 4),))
    w_input_output = normal_values(key_of[5], (D, 2 * N), D ** -0.5, 0.125)
    w_step = normal_values(key_of[6], (D, H), D ** -0.5, 0.125, ((1, 4),))
    conv_value = normal_values(key_of[7], (K, DI), K ** -0.5, 3.0, ((1, 4),), jnp.float32)
    conv_input_output = normal_values(key_of[8], (K, 2 * N), K ** -0.5, 3.0, (), jnp.float32)
    step_bias = jnp.clip(-4.5 + 2.5 * jax.random.uniform(key_of[9], (H,), jnp.float32) ** shard_levels(key_of[9], (H,), ((0, 4),), -0.2, 0.2), -4.5, -2.0)
    log_rate = draw_log_rate(jax.random.fold_in(key_of[13], 71), part)
    skip_gain = jnp.clip(0.5 + 1.0 * jax.random.uniform(key_of[11], (H,), jnp.float32) ** shard_levels(key_of[11], (H,), ((0, 4),), -0.2, 0.2), 0.5, 1.5)
    norm_gain = jnp.clip(1.0 + 0.1 * jax.random.normal(key_of[12], (DI,), jnp.float32), 0.5, 1.5)
    return dict(latent=latent, order=order, inverse=inverse, w_gate=w_gate, w_value=w_value, w_input_output=w_input_output, w_step=w_step, conv_value=conv_value, conv_input_output=conv_input_output, step_bias=step_bias, log_rate=log_rate, skip_gain=skip_gain, norm_gain=norm_gain)


def block_math(x_block, b_block, c_block, step_block, decay_block, state, skip_gain):
    cum_decay = jnp.cumsum(decay_block, axis=0)
    scores = jnp.dot(c_block, b_block.T, preferred_element_type=jnp.float32)
    cum_heads = cum_decay.T
    decay_gap = cum_heads[:, :, None] - cum_heads[:, None, :]
    causal = (lax.iota(jnp.int32, Q)[:, None] >= lax.iota(jnp.int32, Q)[None, :])[None, :, :]
    decay_factor = jnp.exp(jnp.where(causal, decay_gap, -jnp.inf))
    weight = (scores[None, :, :] * decay_factor * step_block.T[:, None, :]).astype(jnp.bfloat16)
    y_local = jnp.einsum('hts,shp->thp', weight.astype(jnp.float32), x_block.astype(jnp.float32))
    to_end = jnp.exp(cum_decay[-1][None, :] - cum_decay) * step_block
    x_scaled = (x_block.astype(jnp.float32) * to_end[:, :, None]).astype(jnp.bfloat16)
    block_state = jnp.einsum('shp,sn->hpn', x_scaled.astype(jnp.float32), b_block.astype(jnp.float32))
    y_carried = jnp.exp(cum_decay)[:, :, None] * jnp.einsum('tn,hpn->thp', c_block.astype(jnp.float32), state, precision=lax.Precision.HIGHEST)
    new_state = jnp.exp(cum_decay[-1])[:, None, None] * state + block_state
    y_total = y_local + y_carried + skip_gain[None, :, None] * x_block.astype(jnp.float32)
    return (y_total, new_state)

def reference(latent, order, inverse, w_gate, w_value, w_input_output, w_step, conv_value, conv_input_output, step_bias, log_rate, skip_gain, norm_gain):
    length = latent.shape[0]
    scan_rows = jnp.zeros_like(latent).at[inverse].set(latent)
    gate_act = jnp.dot(scan_rows, w_gate, preferred_element_type=jnp.float32).astype(jnp.bfloat16)
    conv_in = jnp.concatenate([jnp.dot(scan_rows, w_value, preferred_element_type=jnp.float32), jnp.dot(scan_rows, w_input_output, preferred_element_type=jnp.float32)], axis=1).astype(jnp.bfloat16)
    step_raw = jnp.dot(scan_rows, w_step, preferred_element_type=jnp.float32)
    kernel = jnp.concatenate([conv_value, conv_input_output], axis=1)
    padded = jnp.concatenate([jnp.zeros((K - 1, conv_in.shape[1]), jnp.bfloat16), conv_in], axis=0)
    conv_sum = padded[0:length].astype(jnp.float32) * kernel[0]
    for tap_index in range(1, K):
        conv_sum = conv_sum + padded[tap_index:tap_index + length].astype(jnp.float32) * kernel[tap_index]
    conv_act = jax.nn.silu(conv_sum).astype(jnp.bfloat16)
    x_act = conv_act[:, :DI].reshape(length // Q, Q, H, HEAD)
    b_act = conv_act[:, DI:DI + N].reshape(length // Q, Q, N)
    c_act = conv_act[:, DI + N:].reshape(length // Q, Q, N)
    step_size = jax.nn.softplus(step_raw + step_bias)
    log_decay = -jnp.exp(log_rate) * step_size
    step_blocks = step_size.reshape(length // Q, Q, H)
    decay_blocks = log_decay.reshape(length // Q, Q, H)

    def one_block(state, pieces):
        y_total, new_state = block_math(pieces[0], pieces[1], pieces[2], pieces[3], pieces[4], state, skip_gain)
        return (new_state, y_total)
    start_state = jnp.zeros((H, HEAD, N), jnp.float32)
    final_state, y_blocks = lax.scan(one_block, start_state, (x_act, b_act, c_act, step_blocks, decay_blocks))
    y_total = y_blocks.reshape(length, H, HEAD)
    gated = y_total * jax.nn.silu(gate_act.astype(jnp.float32)).reshape(length, H, HEAD)
    inv_rms = lax.rsqrt(lax.optimization_barrier(jnp.mean(gated * gated, axis=2, keepdims=True)) + 1e-05)
    normed = ((gated * inv_rms).reshape(length, DI) * norm_gain).astype(jnp.bfloat16)
    return jnp.zeros_like(normed).at[order].set(normed)
```

```python
import jax
import jax.numpy as jnp
from jax import lax
from jax.experimental import pallas as pl
from jax.experimental.pallas import tpu as pltpu
from jax.sharding import PartitionSpec as P

F32, BF, I32 = jnp.float32, jnp.bfloat16, jnp.int32
ROWS = 512
SEQ = 16
QUAD = ROWS // 4
SLOT = QUAD + 16
WIN = 32
KEYS = SEQ * WIN
CH = 64
BLOCK = 128
MIB = 1 << 20


def iota(shape, dim):
    return lax.broadcasted_iota(I32, shape, dim)


def dot(a, b, dims=((1,), (0,))):
    return lax.dot_general(a, b, (dims, ((), ())), preferred_element_type=F32)


def column(row):
    return jnp.transpose(jnp.broadcast_to(row, (128, row.shape[1])))


def tiles(row):
    return [row[:, g : g + 128] for g in range(0, row.shape[1], 128)]


def sorted_place(inv, inv_col):
    rank = jnp.concatenate(
        [jnp.sum((inv_col < part).astype(F32), axis=0, keepdims=True) for part in tiles(inv)],
        axis=1,
    )
    packed = jnp.floor(rank * 0.25)
    return (rank - 4.0 * packed) * QUAD + packed


def one_hot(place, count):
    return (iota((count, place.shape[1]), 0) == place.astype(I32)).astype(F32).astype(BF)


def stacked(rows, shape):
    place = iota(shape, 0)
    block = jnp.zeros(shape, F32)
    for index, row in enumerate(rows):
        block = jnp.where(place == index, row, block)
    return block


def side_by_side(low, high):
    first = iota((QUAD, 128), 1) < 64
    return [
        jnp.where(first, low[u : u + QUAD], high[u + QUAD : u + 2 * QUAD]) for u in (0, 2 * QUAD)
    ]


def front_body(at_ref, inv_ref, ord_ref, lat_ref, wio_ref, out_ref):
    inv = inv_ref[...].astype(F32)
    inv_col = column(inv)
    deal = one_hot(sorted_place(inv, inv_col), ROWS)
    io = dot(lat_ref[...], wio_ref[...]).astype(BF)
    io = dot(deal, io)
    m = at_ref[0]
    half = jnp.where(m >= 2, io[:, 128:], io[:, :128])
    turned = pltpu.roll(half, 64, 1)
    odd = m % 2 == 1
    packed = side_by_side(jnp.where(odd, turned, half), jnp.where(odd, half, turned))
    source = (ord_ref[...] >> 9).astype(F32)
    source_col = column(source)
    earlier = [
        jnp.sum(
            jnp.where(
                (source_col == part) & (iota((ROWS, 128), 0) < iota((ROWS, 128), 1) + 128 * g),
                1.0,
                0.0,
            ),
            axis=0,
            keepdims=True,
        )
        for g, part in enumerate(tiles(source))
    ]
    bound = (iota((ROWS, 128), 1) * ROWS).astype(F32)
    start = jnp.sum((inv_col < bound).astype(F32), axis=0, keepdims=True)
    tile = jnp.minimum(jnp.floor(start * (1.0 / 64.0)), 6.0)
    offset = start - 64.0 * tile
    blank = jnp.zeros((1, 128), F32)
    side = stacked(
        [
            source[:, :256],
            source[:, 256:],
            jnp.concatenate(earlier[:2], axis=1),
            jnp.concatenate(earlier[2:], axis=1),
            jnp.concatenate([tile, blank], axis=1),
            jnp.concatenate([offset, blank], axis=1),
        ],
        (16, 256),
    )
    slot = jnp.concatenate([jnp.concatenate(packed, axis=1), side], axis=0).astype(BF)
    for index in range(out_ref.shape[0]):
        out_ref[index] = slot


def value_body(inv_ref, lat_ref, wv_ref, ws_ref, out_ref, deal_ref, step_ref):
    n = pl.program_id(0)

    @pl.when(n == 0)
    def _():
        inv = inv_ref[...].astype(F32)
        deal_ref[...] = one_hot(sorted_place(inv, column(inv)), ROWS)
        rest = dot(ws_ref[...], lat_ref[...], ((1,), (1,)))
        for part in range(3):
            piece = rest.astype(BF)
            step_ref[part] = dot(piece, deal_ref[...], ((1,), (1,)))
            rest = rest - piece.astype(F32)

    value = dot(lat_ref[...], wv_ref[...]).astype(BF)
    value = dot(deal_ref[...], value)
    for jj in range(4):
        group = value[:, 128 * (jj // 2) : 128 * (jj // 2) + 128]
        turned = pltpu.roll(group, 64, 1)
        packed = side_by_side(group, turned) if jj % 2 == 0 else side_by_side(turned, group)
        head = 2 * n + jj // 2
        rows = []
        for part in range(3):
            steps = step_ref[part, pl.ds(head, 1), :]
            rows += [steps[:, :256], steps[:, 256:]]
        side = stacked(rows, (16, 256))
        out_ref[jj] = jnp.concatenate([jnp.concatenate(packed, axis=1), side], axis=0).astype(BF)


def conv_silu(cur, prev, taps):
    ext = jnp.concatenate([prev, cur], axis=1)
    total = cur * taps[3]
    for back in range(1, 4):
        total = total + pltpu.roll(ext, back, 1)[:, 128:] * taps[3 - back]
    return total * (1.0 / (1.0 + jnp.exp(-total)))


def pick_quarter(res, quarter):
    out = jnp.zeros((CH, res.shape[1]), F32)
    for q in range(4):
        out = out + jnp.where(quarter == q, res[CH * q : CH * q + CH], 0.0)
    return out


def bc_body(at_ref, ab_ref, own_ref, oth_ref, conv_ref, out_ref, code_ref, win_ref, tap_ref):
    m, c = at_ref[0], at_ref[1]
    for z in range(8):
        for ref, core in ((own_ref, c), (oth_ref, 1 - c)):
            d = 2 * z + core
            side = ref[z, QUAD:SLOT, :].astype(F32)
            source = jnp.concatenate([side[0:1], side[1:2]], axis=1).astype(I32)
            place = jnp.concatenate([side[2:3], side[3:4]], axis=1).astype(I32)
            for s in range(SEQ):
                j = (s >> 1) + 8 * ((s + c) % 2)
                place = place + jnp.where(source == s, ab_ref[32 * j + 16 + d], 0)
            code_ref[pl.ds(d, 1), :] = source * 128 + place

    group = conv_ref[:, pl.ds(pl.multiple_of(128 * (m // 2), 128), 128)]
    tap_ref[...] = jnp.transpose(stacked([group[k : k + 1] for k in range(4)], (128, 128)))
    tap_cols = tap_ref[pl.ds(pl.multiple_of(64 * (m % 2), 64), 64), :]
    taps = [tap_cols[:, k : k + 1] for k in range(4)]

    def rows_of(d, lo, hi):
        for j in range(SEQ):
            ref = own_ref if j < 8 else oth_ref
            at = pl.multiple_of(16 * ab_ref[32 * j + d], 16)
            win_ref[WIN * j : WIN * j + WIN, :] = ref[j % 8, pl.ds(at, WIN), :]
        code = code_ref[pl.ds(d, 1), :][:, lo:hi]
        source = code >> 7
        j_of = (source >> 1) + 8 * ((source + c) & 1)
        key = j_of * WIN + ((code >> 2) & (WIN - 1))
        spread = one_hot(key, KEYS)
        return pick_quarter(dot(win_ref[...], spread, ((0,), (0,))), code & 3)

    prev = rows_of(jnp.maximum(8 * c - 1, 0), ROWS - 128, ROWS)
    prev = jnp.where(c > 0, prev, 0.0)

    def one(e, prev):
        cur = rows_of(8 * c + e, 0, ROWS)
        act = conv_silu(cur, prev, taps)
        out_ref[:, pl.ds(pl.multiple_of(ROWS * e, ROWS), ROWS)] = act.astype(BF)
        return cur[:, ROWS - 128 :]

    lax.fori_loop(0, 8, one, prev)


def scan_body(
    at_ref,
    ab_ref,
    bias_ref,
    rate_ref,
    skip_ref,
    code_ref,
    x_ref,
    conv_ref,
    own0,
    own1,
    own2,
    own3,
    oth0,
    oth1,
    oth2,
    oth3,
    out_ref,
    bc_ref,
    win_ref,
    stepwin_ref,
    stepcol_ref,
    tap_ref,
    xact_ref,
    step_ref,
    cum_ref,
    acc_ref,
):
    m, c, sq = at_ref[0], at_ref[1], at_ref[2]
    head = sq // 2
    for k, (own, oth) in enumerate(((own0, oth0), (own1, oth1), (own2, oth2), (own3, oth3))):
        at = pl.multiple_of(CH * ((m - k + 4) % 4), CH)
        bc_ref[c, pl.ds(at, CH), :] = own[...]
        bc_ref[1 - c, pl.ds(at, CH), :] = oth[...]

    group = conv_ref[:, pl.ds(pl.multiple_of(128 * head, 128), 128)]
    tap_ref[...] = jnp.transpose(stacked([group[k : k + 1] for k in range(4)], (128, 128)))
    tap_cols = tap_ref[pl.ds(pl.multiple_of(64 * (sq % 2), 64), 64), :]
    taps = [tap_cols[:, k : k + 1] for k in range(4)]

    for s0 in range(0, SEQ, 8):
        blocks = []
        for s in range(s0, s0 + 8):
            side = x_ref[s, QUAD:SLOT, :].astype(F32)
            blocks += [side[0:8, :128], side[0:8, 128:]]
        turned = jnp.transpose(jnp.concatenate(blocks, axis=0))
        for s in range(s0, s0 + 8):
            own = turned if s == s0 else pltpu.roll(turned, 128 - 16 * (s - s0), 1)
            stepcol_ref[s] = own.astype(BF)

    def tile_at(s, d):
        j = (s >> 1) + 8 * ((s + c) % 2)
        return pl.multiple_of(16 * ab_ref[32 * j + d], 16)

    def spread_of(d):
        code = code_ref[pl.ds(d, 1), :]
        key = (code >> 7) * WIN + ((code >> 2) & (WIN - 1))
        return one_hot(key, KEYS), code & 3

    def gather(d, prev):
        for s in range(SEQ):
            at = tile_at(s, d)
            win_ref[WIN * s : WIN * s + WIN, :] = x_ref[s, pl.ds(at, WIN), :]
            stepwin_ref[WIN * s : WIN * s + WIN, :] = stepcol_ref[s, pl.ds(at, WIN), :]
        spread, quarter = spread_of(d)
        cur = pick_quarter(dot(win_ref[...], spread, ((0,), (0,))), quarter)
        act = conv_silu(cur, prev, taps)
        xact_ref[:, pl.ds(pl.multiple_of(ROWS * d, ROWS), ROWS)] = act.astype(BF)
        parts = dot(stepwin_ref[...], spread, ((0,), (0,)))
        step = jnp.zeros((1, ROWS), F32)
        for q in range(4):
            row = (q >> 1) + 8 * (q & 1)
            value = parts[row : row + 1] + parts[row + 2 : row + 3] + parts[row + 4 : row + 5]
            step = step + jnp.where(quarter == q, value, 0.0)
        step_ref[pl.ds(d, 1), :] = step
        return cur[:, ROWS - 128 :]

    lax.fori_loop(0, SEQ, gather, jnp.zeros((CH, 128), F32))

    raw = step_ref[...] + bias_ref[head]
    size = jnp.maximum(raw, 0.0) + jnp.log1p(jnp.exp(-jnp.abs(raw)))
    step_ref[...] = size
    rate = jnp.exp(jnp.full((1, ROWS), rate_ref[head], F32))
    cum = -rate * size
    lane = iota((SEQ, ROWS), 1) % BLOCK
    for shift in (1, 2, 4, 8, 16, 32, 64):
        cum = cum + jnp.where(lane >= shift, pltpu.roll(cum, shift, 1), 0.0)
    cum_ref[...] = cum
    acc_ref[...] = jnp.zeros_like(acc_ref)
    skip = skip_ref[head]
    causal = iota((BLOCK, BLOCK), 0) <= iota((BLOCK, BLOCK), 1)

    def scan(d, state):
        x_all = xact_ref[:, pl.ds(pl.multiple_of(ROWS * d, ROWS), ROWS)]
        bc = bc_ref[d // 8, :, pl.ds(pl.multiple_of(ROWS * (d % 8), ROWS), ROWS)]
        cum_all = cum_ref[pl.ds(d, 1), :]
        size_all = step_ref[pl.ds(d, 1), :]
        ys = []
        for k in range(ROWS // BLOCK):
            at = slice(BLOCK * k, BLOCK * k + BLOCK)
            x = x_all[:, at].astype(F32)
            b, cc = bc[:BLOCK, at], bc[BLOCK:, at]
            cum_row, size = cum_all[:, at], size_all[:, at]
            scores = dot(b, cc, ((0,), (0,)))
            gap = jnp.where(causal, cum_row - column(cum_row), -1e30)
            weight = (scores * jnp.exp(gap)).astype(BF)
            y = dot((x * size).astype(BF), weight)
            y = y + dot(state.astype(BF), cc) * jnp.exp(cum_row) + skip * x
            ys.append(y)
            total = cum_row[:, BLOCK - 1 :]
            scaled = (x * (jnp.exp(total - cum_row) * size)).astype(BF)
            state = jnp.exp(total) * state + dot(scaled, b, ((1,), (1,)))
        y_all = jnp.concatenate(ys, axis=1)
        spread, quarter = spread_of(d)
        apart = jnp.concatenate(
            [jnp.where(quarter == q, y_all, 0.0).astype(BF) for q in range(4)], axis=0
        )
        back = dot(spread, apart, ((1,), (1,)))
        for s in range(SEQ):
            at = pl.ds(tile_at(s, d), WIN)
            acc_ref[s, at, :] = acc_ref[s, at, :] + back[WIN * s : WIN * s + WIN]
        return state

    lax.fori_loop(0, SEQ, scan, jnp.zeros((CH, BLOCK), F32))
    out_ref[...] = acc_ref[...].astype(BF)


def final_body(inv_ref, y_ref, gate_ref, gain_ref, out_ref, pick_ref):
    @pl.when(pl.program_id(0) == 0)
    def _():
        inv = inv_ref[...].astype(F32)
        place = column(sorted_place(inv, column(inv)))
        lane = iota((ROWS, 128), 1)
        for g in range(4):
            hit = place == (lane + 128 * g).astype(F32)
            pick_ref[:, 128 * g : 128 * g + 128] = hit.astype(F32).astype(BF)

    low = iota((QUAD, 128), 1) < 64
    rows = []
    for q in range(4):
        at = slice(128 * (q // 2), 128 * (q // 2) + 128)
        even, odd = y_ref[0, :, at].astype(F32), y_ref[1, :, at].astype(F32)
        if q % 2 == 0:
            rows.append(jnp.where(low, even, pltpu.roll(odd, 64, 1)))
        else:
            rows.append(jnp.where(low, pltpu.roll(even, 64, 1), odd))
    y = dot(pick_ref[...], jnp.concatenate(rows, axis=0).astype(BF))
    gate = gate_ref[...].astype(F32)
    gated = y * (gate * (1.0 / (1.0 + jnp.exp(-gate))))
    mean = jnp.mean(gated * gated, axis=1, keepdims=True)
    out_ref[...] = (gated * lax.rsqrt(mean + 1e-5) * gain_ref[...]).astype(BF)


def vmem(*_):
    return pl.BlockSpec(memory_space=pltpu.VMEM)


def smem(*_):
    return pl.BlockSpec(memory_space=pltpu.SMEM)


def params(mib):
    return pltpu.CompilerParams(vmem_limit_bytes=mib * MIB)


def cost(flops, data, exps=0):
    return pl.CostEstimate(flops=flops, bytes_accessed=data, transcendentals=exps)


def body(
    latent,
    order,
    inverse,
    w_gate,
    w_value,
    w_input_output,
    w_step,
    conv_value,
    conv_input_output,
    step_bias,
    log_rate,
    skip_gain,
    norm_gain,
):
    m, sq = lax.axis_index("mp"), lax.axis_index("seq")
    at = jnp.stack([m, sq % 2, sq, m]).astype(I32)
    inv = inverse.reshape(1, ROWS)
    pairs = [(i, i ^ 1) for i in range(SEQ)]
    lines = [[2 * i + core for i in range(SEQ // 2)] for core in range(2)]

    bc_slots = pl.pallas_call(
        front_body,
        out_shape=jax.ShapeDtypeStruct((8, SLOT, 256), BF),
        in_specs=[smem(), vmem(), vmem(), vmem(), vmem()],
        out_specs=vmem(),
        compiler_params=params(24),
        cost_estimate=cost(1 << 30, 4 << 20),
        name="front",
    )(at, inv, order.reshape(1, ROWS), latent, w_input_output)
    own = lax.all_to_all(bc_slots, "seq", 0, 0, axis_index_groups=lines, tiled=True)

    x_slots = pl.pallas_call(
        value_body,
        grid=(4,),
        out_shape=jax.ShapeDtypeStruct((SEQ, SLOT, 256), BF),
        in_specs=[
            pl.BlockSpec((1, ROWS), lambda n: (0, 0)),
            pl.BlockSpec((ROWS, latent.shape[1]), lambda n: (0, 0)),
            pl.BlockSpec((latent.shape[1], 256), lambda n: (0, n)),
            pl.BlockSpec((8, latent.shape[1]), lambda n: (0, 0)),
        ],
        out_specs=pl.BlockSpec((4, SLOT, 256), lambda n: (n, 0, 0)),
        scratch_shapes=[pltpu.VMEM((ROWS, ROWS), BF), pltpu.VMEM((3, 8, ROWS), F32)],
        compiler_params=params(24),
        cost_estimate=cost(3 << 30, 8 << 20),
        name="value",
    )(inv, latent, w_value, w_step.T)
    gate = jnp.dot(latent, w_gate, preferred_element_type=F32).astype(BF)

    x_slots, own = lax.optimization_barrier((x_slots, own))
    oth = lax.ppermute(own, "seq", pairs)
    x_all = lax.all_to_all(x_slots, "seq", 0, 0, tiled=True)

    side = jnp.concatenate([own[:, QUAD + 4 : QUAD + 6, :16], oth[:, QUAD + 4 : QUAD + 6, :16]], 0)
    ab = side.astype(I32).reshape(-1)
    bc, code = pl.pallas_call(
        bc_body,
        out_shape=(
            jax.ShapeDtypeStruct((CH, 8 * ROWS), BF),
            jax.ShapeDtypeStruct((SEQ, ROWS), I32),
        ),
        in_specs=[smem(), smem(), vmem(), vmem(), vmem()],
        out_specs=(vmem(), vmem()),
        scratch_shapes=[pltpu.VMEM((KEYS, 256), BF), pltpu.VMEM((128, 128), F32)],
        compiler_params=params(24),
        cost_estimate=cost(1 << 30, 2 << 20),
        name="bc",
    )(at, ab, own, oth, conv_input_output)
    owns = [bc] + [
        lax.ppermute(bc, "mp", [(i, (i + k) % 4) for i in range(4)]) for k in range(1, 4)
    ]
    oths = [lax.ppermute(v, "seq", pairs) for v in owns]

    y_slots = pl.pallas_call(
        scan_body,
        out_shape=jax.ShapeDtypeStruct((SEQ, QUAD, 256), BF),
        in_specs=[smem()] * 5 + [vmem()] * 11,
        out_specs=vmem(),
        scratch_shapes=[
            pltpu.VMEM((2, 256, 8 * ROWS), BF),
            pltpu.VMEM((KEYS, 256), BF),
            pltpu.VMEM((KEYS, 128), BF),
            pltpu.VMEM((SEQ, 128, 128), BF),
            pltpu.VMEM((128, 128), F32),
            pltpu.VMEM((CH, SEQ * ROWS), BF),
            pltpu.VMEM((SEQ, ROWS), F32),
            pltpu.VMEM((SEQ, ROWS), F32),
            pltpu.VMEM((SEQ, QUAD, 256), F32),
        ],
        compiler_params=params(32),
        cost_estimate=cost(8 << 30, 8 << 20),
        name="scan",
    )(at, ab, step_bias, log_rate, skip_gain, code, x_all, conv_value, *owns, *oths)
    y_all = lax.all_to_all(y_slots, "seq", 0, 0, tiled=True)

    heads = step_bias.shape[0]
    return pl.pallas_call(
        final_body,
        grid=(heads,),
        out_shape=jax.ShapeDtypeStruct((ROWS, heads * 128), BF),
        in_specs=[
            pl.BlockSpec((1, ROWS), lambda h: (0, 0)),
            pl.BlockSpec((2, QUAD, 256), lambda h: (h, 0, 0)),
            pl.BlockSpec((ROWS, 128), lambda h: (0, h)),
            pl.BlockSpec((1, 128), lambda h: (0, h)),
        ],
        out_specs=pl.BlockSpec((ROWS, 128), lambda h: (0, h)),
        scratch_shapes=[pltpu.VMEM((ROWS, ROWS), BF)],
        compiler_params=params(24),
        cost_estimate=cost(1 << 30, 3 << 20),
        name="final",
    )(inv, y_all, gate, norm_gain.reshape(1, -1))


def solution(mesh):
    return jax.shard_map(
        body,
        mesh=mesh,
        in_specs=(
            P(("batch", "seq"), None),
            P("seq"),
            P("seq"),
            P(None, "mp"),
            P(None, "mp"),
            P(),
            P(None, "mp"),
            P(None, "mp"),
            P(),
            P("mp"),
            P("mp"),
            P("mp"),
            P("mp"),
        ),
        out_specs=P(("batch", "seq"), "mp"),
        check_vma=False,
    )
```

```python
import jax
import jax.numpy as jnp
from jax import lax
from jax.experimental import pallas as pl
from jax.experimental.pallas import tpu as pltpu
from jax.sharding import PartitionSpec as P

F32, BF, I32 = jnp.float32, jnp.bfloat16, jnp.int32
ROWS = 512
SEQ = 16
QUAD = ROWS // 4
SLOT = QUAD + 16
WIN = 32
KEYS = SEQ * WIN
CH = 64
BLOCK = 256
BC = 128
MIB = 1 << 20


def iota(shape, dim):
    return lax.broadcasted_iota(I32, shape, dim)


def dot(a, b, dims=((1,), (0,))):
    return lax.dot_general(a, b, (dims, ((), ())), preferred_element_type=F32)


def column(row):
    return jnp.transpose(jnp.broadcast_to(row, (128, row.shape[1])))


def tiles(row):
    return [row[:, g : g + 128] for g in range(0, row.shape[1], 128)]


def sorted_place(inv, inv_col):
    rank = jnp.concatenate(
        [jnp.sum((inv_col < part).astype(F32), axis=0, keepdims=True) for part in tiles(inv)],
        axis=1,
    )
    packed = jnp.floor(rank * 0.25)
    return (rank - 4.0 * packed) * QUAD + packed


def one_hot(place, count):
    row = iota((count, place.shape[1]), 0).astype(jnp.int16)
    return jnp.where(row == place.astype(I32).astype(jnp.int16), BF(1), BF(0))


def stacked(rows, shape):
    place = iota(shape, 0)
    block = jnp.zeros(shape, F32)
    for index, row in enumerate(rows):
        block = jnp.where(place == index, row, block)
    return block


def side_by_side(low, high):
    first = iota((QUAD, 128), 1) < 64
    return [
        jnp.where(first, low[u : u + QUAD], high[u + QUAD : u + 2 * QUAD]) for u in (0, 2 * QUAD)
    ]


def front_body(
    at_ref,
    inv_hbm,
    ord_hbm,
    lat_hbm,
    wio_hbm,
    ws_ref,
    out_ref,
    inv_ref,
    ord_ref,
    lat_ref,
    wio_ref,
    sem_ref,
):
    small = [
        pltpu.make_async_copy(inv_hbm, inv_ref, sem_ref.at[0]),
        pltpu.make_async_copy(ord_hbm, ord_ref, sem_ref.at[1]),
    ]
    large = []
    for k in range(4):
        part = pl.ds(512 * k, 512)
        large.append(
            (
                pltpu.make_async_copy(lat_hbm.at[:, part], lat_ref.at[:, part], sem_ref.at[2 + k]),
                pltpu.make_async_copy(wio_hbm.at[part], wio_ref.at[part], sem_ref.at[6 + k]),
            )
        )
    for copy in small:
        copy.start()
    for pair in large:
        for copy in pair:
            copy.start()
    for copy in small:
        copy.wait()
    inv = inv_ref[...].astype(F32)
    inv_col = column(inv)
    deal = one_hot(sorted_place(inv, inv_col), ROWS)
    source = (ord_ref[...] >> 9).astype(F32)
    source_col = column(source)
    earlier = [
        jnp.sum(
            jnp.where(
                (source_col == part) & (iota((ROWS, 128), 0) < iota((ROWS, 128), 1) + 128 * g),
                1.0,
                0.0,
            ),
            axis=0,
            keepdims=True,
        )
        for g, part in enumerate(tiles(source))
    ]
    bound = (iota((ROWS, 128), 1) * ROWS).astype(F32)
    start = jnp.sum((inv_col < bound).astype(F32), axis=0, keepdims=True)
    tile = jnp.minimum(jnp.floor(start * (1.0 / 64.0)), 6.0)
    offset = start - 64.0 * tile
    blank = jnp.zeros((1, 128), F32)
    rows = [
        source[:, :256],
        source[:, 256:],
        jnp.concatenate(earlier[:2], axis=1),
        jnp.concatenate(earlier[2:], axis=1),
        jnp.concatenate([tile, blank], axis=1),
        jnp.concatenate([offset, blank], axis=1),
    ]
    io = jnp.zeros((ROWS, 256), F32)
    rest = jnp.zeros((ROWS, 128), F32)
    ws = jnp.concatenate([ws_ref[...], jnp.zeros((120, ws_ref.shape[1]), BF)], axis=0)
    for k, pair in enumerate(large):
        for copy in pair:
            copy.wait()
        part = slice(512 * k, 512 * k + 512)
        io = io + dot(lat_ref[:, part], wio_ref[part, :])
        rest = rest + dot(lat_ref[:, part], ws[:, part], ((1,), (1,)))
    io = dot(deal, io.astype(BF))
    rest = jnp.transpose(rest)[:8]
    pieces = []
    for _ in range(3):
        piece = rest.astype(BF)
        pieces.append(piece.astype(F32))
        rest = rest - pieces[-1]
    pieces = jnp.concatenate(pieces + [rest], axis=0).astype(BF)
    dealt = dot(pieces, deal, ((1,), (1,)))
    steps = [dealt[8 * k : 8 * k + 8] for k in range(3)]
    m = at_ref[0]
    half = jnp.where(m >= 2, io[:, 128:], io[:, :128])
    turned = pltpu.roll(half, 64, 1)
    odd = m % 2 == 1
    packed = side_by_side(jnp.where(odd, turned, half), jnp.where(odd, half, turned))
    slot = jnp.concatenate(packed, axis=1).astype(BF)
    for head in range(out_ref.shape[0]):
        halves = []
        for step in steps:
            own = step[head : head + 1]
            halves += [own[:, :256], own[:, 256:]]
        out_ref[head, :QUAD, :] = slot
        out_ref[head, QUAD:, :] = stacked(rows + halves, (16, 256)).astype(BF)


def value_body(inv_ref, lat_ref, wv_ref, out_ref, deal_ref):
    @pl.when(pl.program_id(0) == 0)
    def _():
        inv = inv_ref[...].astype(F32)
        deal_ref[...] = one_hot(sorted_place(inv, column(inv)), ROWS)

    value = dot(lat_ref[...], wv_ref[...]).astype(BF)
    value = dot(deal_ref[...], value)
    for jj in range(4):
        group = value[:, 128 * (jj // 2) : 128 * (jj // 2) + 128]
        turned = pltpu.roll(group, 64, 1)
        packed = side_by_side(group, turned) if jj % 2 == 0 else side_by_side(turned, group)
        out_ref[jj] = jnp.concatenate(packed, axis=1).astype(BF)


def silu(x):
    half = 0.5 * x
    return half + half * jnp.tanh(half)


def conv_silu(cur, prev, taps):
    ext = jnp.concatenate([prev, cur], axis=1)
    total = cur * taps[3]
    for back in range(1, 4):
        total = total + pltpu.roll(ext, back, 1)[:, 128:] * taps[3 - back]
    return silu(total)


def pick_quarter(res, quarter):
    out = jnp.zeros((CH, res.shape[1]), F32)
    for q in range(4):
        out = out + jnp.where(quarter == q, res[CH * q : CH * q + CH], 0.0)
    return out


def code_body(at_ref, ab_ref, own_ref, oth_ref, code_ref):
    c = at_ref[1]
    for z in range(8):
        for ref, core in ((own_ref, c), (oth_ref, 1 - c)):
            d = 2 * z + core
            side = ref[z, QUAD:SLOT, :].astype(F32)
            source = jnp.concatenate([side[0:1], side[1:2]], axis=1).astype(I32)
            place = jnp.concatenate([side[2:3], side[3:4]], axis=1).astype(I32)
            for s in range(SEQ):
                j = (s >> 1) + 8 * ((s + c) % 2)
                place = place + jnp.where(source == s, ab_ref[32 * j + 16 + d], 0)
            code_ref[pl.ds(d, 1), :] = source * 128 + place


def bc_body(
    at_ref, ab_ref, own_ref, oth_ref, conv_ref, out_a, out_b, code_ref, win_ref, tap_ref
):
    code_body(at_ref, ab_ref, own_ref, oth_ref, code_ref)
    m, c = at_ref[0], at_ref[1]
    group = conv_ref[:, pl.ds(pl.multiple_of(128 * (m // 2), 128), 128)]
    tap_ref[...] = jnp.transpose(stacked([group[k : k + 1] for k in range(4)], (128, 128)))
    tap_cols = tap_ref[pl.ds(pl.multiple_of(64 * (m % 2), 64), 64), :]
    taps = [tap_cols[:, k : k + 1] for k in range(4)]

    def rows_of(d, lo, hi):
        for j in range(SEQ):
            ref = own_ref if j < 8 else oth_ref
            at = pl.multiple_of(16 * ab_ref[32 * j + d], 16)
            win_ref[WIN * j : WIN * j + WIN, :] = ref[j % 8, pl.ds(at, WIN), :]
        code = code_ref[pl.ds(d, 1), :][:, lo:hi]
        source = code >> 7
        j_of = (source >> 1) + 8 * ((source + c) & 1)
        key = j_of * WIN + ((code >> 2) & (WIN - 1))
        spread = one_hot(key, KEYS)
        return pick_quarter(dot(win_ref[...], spread, ((0,), (0,))), code & 3)

    first = 8 * c
    prev = rows_of(jnp.maximum(first - 1, 0), ROWS - 128, ROWS)
    prev = jnp.where(first > 0, prev, 0.0)

    for e in range(8):
        cur = rows_of(first + e, 0, ROWS)
        out_ref = out_a if e < 4 else out_b
        out_ref[:, ROWS * (e % 4) : ROWS * (e % 4) + ROWS] = conv_silu(cur, prev, taps).astype(BF)
        prev = cur[:, ROWS - 128 :]


def tile_at(ab_ref, c, s, d):
    j = (s >> 1) + 8 * ((s + c) % 2)
    return pl.multiple_of(16 * ab_ref[32 * j + d], 16)


def time_body(
    at_ref, ab_ref, bias_ref, rate_ref, skip_ref, code_ref, own_ref, oth_ref, conv_ref,
    table_ref, win_ref, col_ref, step_ref, tap_ref
):
    c, sq = at_ref[1], at_ref[2]
    head = sq // 2
    group = conv_ref[:, pl.ds(pl.multiple_of(128 * head, 128), 128)]
    tap_ref[...] = jnp.transpose(stacked([group[k : k + 1] for k in range(4)], (128, 128)))
    table_ref[64:, :128] = tap_ref[pl.ds(pl.multiple_of(64 * (sq % 2), 64), 64), :]
    table_ref[0:SEQ, :] = code_ref[...].astype(F32)
    table_ref[48:64, :] = jnp.full((16, ROWS), skip_ref[head], F32)
    for core, ref in enumerate((own_ref, oth_ref)):
        blocks = []
        for z in range(8):
            side = ref[z, QUAD:SLOT, :].astype(F32)
            side = pltpu.roll(side, 10, 0)[0:8]
            blocks += [side[:, :128], side[:, 128:]]
        turned = jnp.transpose(jnp.concatenate(blocks, axis=0))
        for z in range(8):
            own = turned if z == 0 else pltpu.roll(turned, 128 - 16 * z, 1)
            col_ref[8 * core + z] = own.astype(BF)

    def gather(d, carry):
        for j in range(SEQ):
            at = pl.multiple_of(16 * ab_ref[32 * j + d], 16)
            win_ref[WIN * j : WIN * j + WIN, :] = col_ref[j, pl.ds(at, WIN), :]
        code = code_ref[pl.ds(d, 1), :]
        source = code >> 7
        j_of = (source >> 1) + 8 * ((source + c) & 1)
        spread = one_hot(j_of * WIN + ((code >> 2) & (WIN - 1)), KEYS)
        quarter = code & 3
        parts = dot(win_ref[...], spread, ((0,), (0,)))
        step = jnp.zeros((1, ROWS), F32)
        for q in range(4):
            row = (q >> 1) + 8 * (q & 1)
            value = parts[row : row + 1] + parts[row + 2 : row + 3] + parts[row + 4 : row + 5]
            step = step + jnp.where(quarter == q, value, 0.0)
        step_ref[pl.ds(d, 1), :] = step
        return carry

    lax.fori_loop(0, SEQ, gather, 0, unroll=4)

    raw = step_ref[...] + bias_ref[head]
    size = jnp.maximum(raw, 0.0) + jnp.log1p(jnp.exp(-jnp.abs(raw)))
    table_ref[SEQ : 2 * SEQ, :] = size
    rate = jnp.exp(jnp.full((1, ROWS), rate_ref[head], F32))
    cum = -rate * size
    lane = iota((SEQ, ROWS), 1) & (BLOCK - 1)
    shift = 1
    while shift < BLOCK:
        cum = cum + jnp.where(lane >= shift, pltpu.roll(cum, shift, 1), 0.0)
        shift *= 2
    table_ref[2 * SEQ : 3 * SEQ, :] = cum


def gate_body(lat_ref, w_ref, out_ref):
    out_ref[...] = silu(dot(lat_ref[...], w_ref[...])).astype(BF)


def spread_of(table_ref, d):
    code = table_ref[pl.ds(d, 1), :].astype(I32)
    return one_hot((code >> 7) * WIN + ((code >> 2) & (WIN - 1)), KEYS), code & 3


def place_half(first, prev, at_ref, ab_ref, table_ref, x_ref, xact_ref, win_ref):
    c = at_ref[1]
    taps = [table_ref[64:, k : k + 1] for k in range(4)]

    def gather(e, prev):
        d = first + e
        for s in range(SEQ):
            at = tile_at(ab_ref, c, s, d)
            win_ref[WIN * s : WIN * s + WIN, :] = x_ref[s, pl.ds(at, WIN), :]
        spread, quarter = spread_of(table_ref, d)
        cur = pick_quarter(dot(win_ref[...], spread, ((0,), (0,))), quarter)
        act = conv_silu(cur, prev, taps)
        xact_ref[:, pl.ds(pl.multiple_of(ROWS * e, ROWS), ROWS)] = act.astype(BF)
        return cur[:, ROWS - 128 :]

    return lax.fori_loop(0, SEQ // 2, gather, prev, unroll=4)


def place_first(at_ref, ab_ref, table_ref, x_ref, xact_ref, last_ref, win_ref):
    prev = jnp.zeros((CH, 128), F32)
    last_ref[...] = place_half(0, prev, at_ref, ab_ref, table_ref, x_ref, xact_ref, win_ref)


def place_second(at_ref, ab_ref, table_ref, x_ref, last_ref, xact_ref, win_ref):
    place_half(8, last_ref[...], at_ref, ab_ref, table_ref, x_ref, xact_ref, win_ref)


def scan_body(at_ref, ab_ref, table_ref, xact_a, xact_b, *refs):
    owns, oths = refs[:8], refs[8:16]
    out_ref, bc_ref, acc_ref, sem_ref = refs[16:]
    m, c = at_ref[0], at_ref[1]
    copies = []
    for index in range(8):
        rows = pl.ds(pl.multiple_of(CH * ((m - index // 2 + 4) % 4), CH), CH)
        cols = pl.ds(4 * ROWS * (index % 2), 4 * ROWS)
        for side, ref in enumerate((owns[index], oths[index])):
            half = c if side == 0 else 1 - c
            copies.append(
                pltpu.make_async_copy(ref, bc_ref.at[half, rows, cols], sem_ref.at[index, side])
            )
    for copy in copies:
        copy.start()
    acc_ref[...] = jnp.zeros_like(acc_ref)
    skip = table_ref[48:49, :BLOCK]
    causal = iota((BLOCK, BLOCK), 0) <= iota((BLOCK, BLOCK), 1)
    for copy in copies:
        copy.wait()

    def scan(half, e, state):
        d = 8 * half + e
        cols = pl.ds(pl.multiple_of(ROWS * e, ROWS), ROWS)
        x_all = (xact_b if half else xact_a)[:, cols].astype(F32)
        bc = bc_ref[half, :, cols]
        size_all = table_ref[pl.ds(SEQ + d, 1), :]
        cum_all = table_ref[pl.ds(2 * SEQ + d, 1), :]
        ys = []
        for k in range(ROWS // BLOCK):
            at = slice(BLOCK * k, BLOCK * k + BLOCK)
            x, b, cc = x_all[:, at], bc[:BC, at], bc[BC:, at]
            cum_row, size = cum_all[:, at], size_all[:, at]
            scores = dot(b, cc, ((0,), (0,)))
            col = column(cum_row)
            gap = cum_row - jnp.concatenate([col] * (BLOCK // 128), axis=1)
            weight = (scores * jnp.exp(jnp.where(causal, gap, -1e30))).astype(BF)
            y = dot((x * size).astype(BF), weight)
            y = y + dot(state.astype(BF), cc) * jnp.exp(cum_row) + skip * x
            ys.append(y)
            total = cum_row[:, BLOCK - 1 :]
            scaled = (x * (jnp.exp(total - cum_row) * size)).astype(BF)
            state = jnp.exp(total) * state + dot(scaled, b, ((1,), (1,)))
        y_all = jnp.concatenate(ys, axis=1)
        spread, quarter = spread_of(table_ref, d)
        apart = jnp.concatenate(
            [jnp.where(quarter == q, y_all, 0.0).astype(BF) for q in range(4)], axis=0
        )
        back = dot(spread, apart, ((1,), (1,)))
        for s in range(SEQ):
            at = pl.ds(tile_at(ab_ref, c, s, d), WIN)
            acc_ref[s, at, :] = acc_ref[s, at, :] + back[WIN * s : WIN * s + WIN]
        return state

    state = jnp.zeros((CH, BC), F32)
    for half in range(2):
        state = lax.fori_loop(0, 8, lambda e, state, half=half: scan(half, e, state), state, unroll=4)
    out_ref[...] = acc_ref[...].astype(BF)


def final_body(inv_ref, y_ref, gate_hbm, gain_ref, out_ref, pick_ref, gate_ref, sem_ref):
    h = pl.program_id(0)

    def gate_copy(n):
        part = pl.ds(pl.multiple_of(256 * n, 256), 256)
        return pltpu.make_async_copy(gate_hbm.at[:, part], gate_ref.at[n], sem_ref.at[n])

    @pl.when(h == 0)
    def _():
        for n in range(gate_ref.shape[0]):
            gate_copy(n).start()
        inv = inv_ref[...].astype(F32)
        place = column(sorted_place(inv, column(inv)))
        lane = iota((ROWS, 128), 1)
        for g in range(4):
            hit = place == (lane + 128 * g).astype(F32)
            pick_ref[:, 128 * g : 128 * g + 128] = hit.astype(F32).astype(BF)

    low = iota((QUAD, 128), 1) < 64
    heads = []
    for n in range(2):
        rows = []
        for q in range(4):
            at = slice(128 * (q // 2), 128 * (q // 2) + 128)
            even = y_ref[4 * h + 2 * n, :, at].astype(F32)
            odd = y_ref[4 * h + 2 * n + 1, :, at].astype(F32)
            if q % 2 == 0:
                rows.append(jnp.where(low, even, pltpu.roll(odd, 64, 1)))
            else:
                rows.append(jnp.where(low, pltpu.roll(even, 64, 1), odd))
        heads.append(jnp.concatenate(rows, axis=0).astype(BF))
    y = dot(pick_ref[...], jnp.concatenate(heads, axis=1))
    gate_copy(h).wait()
    for n in range(2):
        at = slice(128 * n, 128 * n + 128)
        gated = y[:, at] * gate_ref[h, :, at].astype(F32)
        mean = jnp.mean(gated * gated, axis=1, keepdims=True)
        out_ref[:, at] = (gated * lax.rsqrt(mean + 1e-5) * gain_ref[:, at]).astype(BF)


def vmem(*_):
    return pl.BlockSpec(memory_space=pltpu.VMEM)


def hbm(*_):
    return pl.BlockSpec(memory_space=pl.ANY)


def smem(*_):
    return pl.BlockSpec(memory_space=pltpu.SMEM)


def params(mib):
    return pltpu.CompilerParams(vmem_limit_bytes=mib * MIB)


def cost(flops, data, exps=0):
    return pl.CostEstimate(flops=flops, bytes_accessed=data, transcendentals=exps)


def run_time(*args):
    return pl.pallas_call(
        time_body,
        out_shape=jax.ShapeDtypeStruct((128, ROWS), F32),
        in_specs=[smem()] * 5 + [vmem()] * 4,
        out_specs=vmem(),
        scratch_shapes=[
            pltpu.VMEM((KEYS, 128), BF),
            pltpu.VMEM((SEQ, 128, 128), BF),
            pltpu.VMEM((SEQ, ROWS), F32),
            pltpu.VMEM((128, 128), F32),
        ],
        compiler_params=params(8),
        cost_estimate=cost(2 << 30, 2 << 20),
        name="time",
    )(*args)


def run_place(kernel, outs, *args):
    return pl.pallas_call(
        kernel,
        out_shape=outs,
        in_specs=[smem()] * 2 + [vmem()] * (len(args) - 2),
        out_specs=tuple(vmem() for _ in outs),
        scratch_shapes=[pltpu.VMEM((KEYS, 256), BF)],
        compiler_params=params(24),
        cost_estimate=cost(2 << 30, 2 << 20),
        name="place",
    )(*args)


def run_scan(*args):
    return pl.pallas_call(
        scan_body,
        out_shape=jax.ShapeDtypeStruct((SEQ, QUAD, 256), BF),
        in_specs=[smem()] * 2 + [vmem()] * 3 + [hbm()] * 16,
        out_specs=vmem(),
        scratch_shapes=[
            pltpu.VMEM((2, 256, 8 * ROWS), BF),
            pltpu.VMEM((SEQ, QUAD, 256), F32),
            pltpu.SemaphoreType.DMA((8, 2)),
        ],
        compiler_params=params(24),
        cost_estimate=cost(8 << 30, 8 << 20),
        name="scan",
    )(*args)


def run_front(*args):
    return pl.pallas_call(
        front_body,
        out_shape=jax.ShapeDtypeStruct((8, SLOT, 256), BF),
        in_specs=[smem(), hbm(), hbm(), hbm(), hbm(), vmem()],
        out_specs=vmem(),
        scratch_shapes=[
            pltpu.VMEM((1, ROWS), I32),
            pltpu.VMEM((1, ROWS), I32),
            pltpu.VMEM(args[3].shape, BF),
            pltpu.VMEM(args[4].shape, BF),
            pltpu.SemaphoreType.DMA((10,)),
        ],
        compiler_params=params(60),
        cost_estimate=cost(1 << 30, 4 << 20),
        name="front",
    )(*args)


def body(
    latent,
    order,
    inverse,
    w_gate,
    w_value,
    w_input_output,
    w_step,
    conv_value,
    conv_input_output,
    step_bias,
    log_rate,
    skip_gain,
    norm_gain,
):
    m, sq = lax.axis_index("mp"), lax.axis_index("seq")
    at = jnp.stack([m, sq % 2, sq, m]).astype(I32)
    inv = inverse.reshape(1, ROWS)
    pairs = [(i, i ^ 1) for i in range(SEQ)]
    lines = [[2 * i + core for i in range(SEQ // 2)] for core in range(2)]

    bc_slots = run_front(at, inv, order.reshape(1, ROWS), latent, w_input_output, w_step.T)
    own = lax.all_to_all(bc_slots, "seq", 0, 0, axis_index_groups=lines, tiled=True)

    x_slots = pl.pallas_call(
        value_body,
        grid=(4,),
        out_shape=jax.ShapeDtypeStruct((SEQ, QUAD, 256), BF),
        in_specs=[
            pl.BlockSpec((1, ROWS), lambda n: (0, 0)),
            pl.BlockSpec((ROWS, latent.shape[1]), lambda n: (0, 0)),
            pl.BlockSpec((latent.shape[1], 256), lambda n: (0, n)),
        ],
        out_specs=pl.BlockSpec((4, QUAD, 256), lambda n: (n, 0, 0)),
        scratch_shapes=[pltpu.VMEM((ROWS, ROWS), BF)],
        compiler_params=params(24),
        cost_estimate=cost(3 << 30, 8 << 20),
        name="value",
    )(inv, latent, w_value)
    gate = pl.pallas_call(
        gate_body,
        grid=(4,),
        out_shape=jax.ShapeDtypeStruct((ROWS, w_gate.shape[1]), BF),
        in_specs=[
            pl.BlockSpec((ROWS, latent.shape[1]), lambda n: (0, 0)),
            pl.BlockSpec((latent.shape[1], 256), lambda n: (0, n)),
        ],
        out_specs=pl.BlockSpec((ROWS, 256), lambda n: (0, n)),
        compiler_params=params(24),
        cost_estimate=cost(2 << 30, 8 << 20),
        name="gate",
    )(latent, w_gate)

    x_slots, own = lax.optimization_barrier((x_slots, own))
    oth = lax.ppermute(own, "seq", pairs)
    x_all = lax.all_to_all(x_slots, "seq", 0, 0, tiled=True)

    side = jnp.concatenate([own[:, QUAD + 4 : QUAD + 6, :16], oth[:, QUAD + 4 : QUAD + 6, :16]], 0)
    ab = side.astype(I32).reshape(-1)
    half = jax.ShapeDtypeStruct((CH, 4 * ROWS), BF)
    bc_a, bc_b, code = pl.pallas_call(
        bc_body,
        out_shape=(half, half, jax.ShapeDtypeStruct((SEQ, ROWS), I32)),
        in_specs=[smem(), smem(), vmem(), vmem(), vmem()],
        out_specs=(vmem(), vmem(), vmem()),
        scratch_shapes=[pltpu.VMEM((KEYS, 256), BF), pltpu.VMEM((128, 128), F32)],
        compiler_params=params(8),
        cost_estimate=cost(1 << 30, 2 << 20),
        name="bc",
    )(at, ab, own, oth, conv_input_output)
    up = [(i, (i + 1) % 4) for i in range(4)]
    down = [(i, (i - 1) % 4) for i in range(4)]
    one_a, three_b = lax.ppermute(bc_a, "mp", up), lax.ppermute(bc_b, "mp", down)
    one_b, three_a = lax.ppermute(bc_b, "mp", up), lax.ppermute(bc_a, "mp", down)
    table = run_time(at, ab, step_bias, log_rate, skip_gain, code, own, oth, conv_value)
    one_a, three_b, table = lax.optimization_barrier((one_a, three_b, table))
    two_a, two_b = lax.ppermute(one_a, "mp", up), lax.ppermute(three_b, "mp", down)
    owns = [bc_a, bc_b, one_a, one_b, two_a, two_b, three_a, three_b]
    part = jax.ShapeDtypeStruct((CH, 8 * ROWS), BF)
    last = jax.ShapeDtypeStruct((CH, 128), F32)
    xact_a, last = run_place(place_first, (part, last), at, ab, table, x_all)
    owns, xact_a = lax.optimization_barrier((owns, xact_a))
    oths = [lax.ppermute(v, "seq", pairs) for v in owns]
    (xact_b,) = run_place(place_second, (part,), at, ab, table, x_all, last)
    y_slots = run_scan(at, ab, table, xact_a, xact_b, *owns, *oths)
    y_all = lax.all_to_all(y_slots, "seq", 0, 0, tiled=True)

    heads = step_bias.shape[0]
    return pl.pallas_call(
        final_body,
        grid=(heads // 2,),
        out_shape=jax.ShapeDtypeStruct((ROWS, heads * 128), BF),
        in_specs=[
            pl.BlockSpec((1, ROWS), lambda h: (0, 0)),
            vmem(),
            hbm(),
            pl.BlockSpec((1, 256), lambda h: (0, h)),
        ],
        out_specs=pl.BlockSpec((ROWS, 256), lambda h: (0, h)),
        scratch_shapes=[
            pltpu.VMEM((ROWS, ROWS), BF),
            pltpu.VMEM((heads // 2, ROWS, 256), BF),
            pltpu.SemaphoreType.DMA((heads // 2,)),
        ],
        compiler_params=params(12),
        cost_estimate=cost(1 << 30, 3 << 20),
        name="final",
    )(inv, y_all, gate, norm_gain.reshape(1, -1))


def solution(mesh):
    return jax.shard_map(
        body,
        mesh=mesh,
        in_specs=(
            P(("batch", "seq"), None),
            P("seq"),
            P("seq"),
            P(None, "mp"),
            P(None, "mp"),
            P(),
            P(None, "mp"),
            P(None, "mp"),
            P(),
            P("mp"),
            P("mp"),
            P("mp"),
            P("mp"),
        ),
        out_specs=P(("batch", "seq"), "mp"),
        check_vma=False,
    )
```

```python
import jax
import jax.numpy as jnp
from jax import lax
from jax.experimental import pallas as pl
from jax.experimental.pallas import tpu as pltpu
from jax.sharding import PartitionSpec as P

F32, BF, I32 = jnp.float32, jnp.bfloat16, jnp.int32
ROWS = 512
SEQ = 16
QUAD = ROWS // 4
SLOT = QUAD + 16
WIN = 32
KEYS = SEQ * WIN
CH = 64
BLOCK = 256
BC = 128
MIB = 1 << 20


def iota(shape, dim):
    return lax.broadcasted_iota(I32, shape, dim)


def dot(a, b, dims=((1,), (0,))):
    return lax.dot_general(a, b, (dims, ((), ())), preferred_element_type=F32)


def column(row):
    return jnp.transpose(jnp.broadcast_to(row, (128, row.shape[1])))


def tiles(row):
    return [row[:, g : g + 128] for g in range(0, row.shape[1], 128)]


def sorted_place(inv, inv_col):
    rank = jnp.concatenate(
        [jnp.sum((inv_col < part).astype(F32), axis=0, keepdims=True) for part in tiles(inv)],
        axis=1,
    )
    packed = jnp.floor(rank * 0.25)
    return (rank - 4.0 * packed) * QUAD + packed


def one_hot(place, count):
    row = iota((count, place.shape[1]), 0).astype(jnp.int16)
    return jnp.where(row == place.astype(I32).astype(jnp.int16), BF(1), BF(0))


def stacked(rows, shape):
    place = iota(shape, 0)
    block = jnp.zeros(shape, F32)
    for index, row in enumerate(rows):
        block = jnp.where(place == index, row, block)
    return block


def side_by_side(low, high):
    first = iota((QUAD, 128), 1) < 64
    return [
        jnp.where(first, low[u : u + QUAD], high[u + QUAD : u + 2 * QUAD]) for u in (0, 2 * QUAD)
    ]


def front_body(
    inv_hbm,
    ord_hbm,
    lat_hbm,
    wio_hbm,
    ws_ref,
    out_ref,
    inv_ref,
    ord_ref,
    lat_ref,
    wio_ref,
    sem_ref,
):
    small = [
        pltpu.make_async_copy(inv_hbm, inv_ref, sem_ref.at[0]),
        pltpu.make_async_copy(ord_hbm, ord_ref, sem_ref.at[1]),
    ]
    large = []
    for k in range(4):
        part = pl.ds(512 * k, 512)
        large.append(
            (
                pltpu.make_async_copy(lat_hbm.at[:, part], lat_ref.at[:, part], sem_ref.at[2 + k]),
                pltpu.make_async_copy(wio_hbm.at[part], wio_ref.at[part], sem_ref.at[6 + k]),
            )
        )
    for copy in small:
        copy.start()
    for pair in large:
        for copy in pair:
            copy.start()
    for copy in small:
        copy.wait()
    inv = inv_ref[...].astype(F32)
    inv_col = column(inv)
    deal = one_hot(sorted_place(inv, inv_col), ROWS)
    source = (ord_ref[...] >> 9).astype(F32)
    source_col = column(source)
    earlier = [
        jnp.sum(
            jnp.where(
                (source_col == part) & (iota((ROWS, 128), 0) < iota((ROWS, 128), 1) + 128 * g),
                1.0,
                0.0,
            ),
            axis=0,
            keepdims=True,
        )
        for g, part in enumerate(tiles(source))
    ]
    bound = (iota((ROWS, 128), 1) * ROWS).astype(F32)
    start = jnp.sum((inv_col < bound).astype(F32), axis=0, keepdims=True)
    tile = jnp.minimum(jnp.floor(start * (1.0 / 64.0)), 6.0)
    offset = start - 64.0 * tile
    blank = jnp.zeros((1, 128), F32)
    rows = [
        source[:, :256],
        source[:, 256:],
        jnp.concatenate(earlier[:2], axis=1),
        jnp.concatenate(earlier[2:], axis=1),
        jnp.concatenate([tile, blank], axis=1),
        jnp.concatenate([offset, blank], axis=1),
    ]
    io = jnp.zeros((ROWS, 256), F32)
    rest = jnp.zeros((ROWS, 128), F32)
    ws = jnp.concatenate([ws_ref[...], jnp.zeros((120, ws_ref.shape[1]), BF)], axis=0)
    for k, pair in enumerate(large):
        for copy in pair:
            copy.wait()
        part = slice(512 * k, 512 * k + 512)
        io = io + dot(lat_ref[:, part], wio_ref[part, :])
        rest = rest + dot(lat_ref[:, part], ws[:, part], ((1,), (1,)))
    io = dot(deal, io.astype(BF))
    rest = jnp.transpose(rest)[:8]
    pieces = []
    for _ in range(3):
        piece = rest.astype(BF)
        pieces.append(piece.astype(F32))
        rest = rest - pieces[-1]
    pieces = jnp.concatenate(pieces + [rest], axis=0).astype(BF)
    dealt = dot(pieces, deal, ((1,), (1,)))
    steps = [dealt[8 * k : 8 * k + 8] for k in range(3)]
    m = lax.axis_index("mp")
    half = jnp.where(m >= 2, io[:, 128:], io[:, :128])
    turned = pltpu.roll(half, 64, 1)
    odd = m % 2 == 1
    packed = side_by_side(jnp.where(odd, turned, half), jnp.where(odd, half, turned))
    slot = jnp.concatenate(packed, axis=1).astype(BF)
    for head in range(out_ref.shape[0]):
        halves = []
        for step in steps:
            own = step[head : head + 1]
            halves += [own[:, :256], own[:, 256:]]
        out_ref[head, :QUAD, :] = slot
        out_ref[head, QUAD:, :] = stacked(rows + halves, (16, 256)).astype(BF)


def value_body(inv_ref, lat_ref, wv_ref, out_ref, deal_ref):
    @pl.when(pl.program_id(0) == 0)
    def _():
        inv = inv_ref[...].astype(F32)
        deal_ref[...] = one_hot(sorted_place(inv, column(inv)), ROWS)

    value = dot(lat_ref[...], wv_ref[...]).astype(BF)
    value = dot(deal_ref[...], value)
    for jj in range(4):
        group = value[:, 128 * (jj // 2) : 128 * (jj // 2) + 128]
        turned = pltpu.roll(group, 64, 1)
        packed = side_by_side(group, turned) if jj % 2 == 0 else side_by_side(turned, group)
        out_ref[jj] = jnp.concatenate(packed, axis=1).astype(BF)


def silu(x):
    half = 0.5 * x
    return half + half * jnp.tanh(half)


def conv_silu(cur, prev, taps):
    ext = jnp.concatenate([prev, cur], axis=1)
    total = cur * taps[3]
    for back in range(1, 4):
        total = total + pltpu.roll(ext, back, 1)[:, 128:] * taps[3 - back]
    return silu(total)


def pick_quarter(res, quarter):
    out = jnp.zeros((CH, res.shape[1]), F32)
    for q in range(4):
        out = out + jnp.where(quarter == q, res[CH * q : CH * q + CH], 0.0)
    return out


def code_body(at_ref, ab_ref, own_ref, oth_ref, code_ref):
    c = at_ref[1]
    for z in range(8):
        for ref, core in ((own_ref, c), (oth_ref, 1 - c)):
            d = 2 * z + core
            side = ref[z, QUAD:SLOT, :].astype(F32)
            source = jnp.concatenate([side[0:1], side[1:2]], axis=1).astype(I32)
            place = jnp.concatenate([side[2:3], side[3:4]], axis=1).astype(I32)
            for s in range(SEQ):
                j = (s >> 1) + 8 * ((s + c) % 2)
                place = place + jnp.where(source == s, ab_ref[32 * j + 16 + d], 0)
            code_ref[pl.ds(d, 1), :] = source * 128 + place


def bc_body(
    at_ref, ab_ref, own_ref, oth_ref, conv_ref, out_a, out_b, code_ref, win_ref, tap_ref
):
    code_body(at_ref, ab_ref, own_ref, oth_ref, code_ref)
    m, c = at_ref[0], at_ref[1]
    group = conv_ref[:, pl.ds(pl.multiple_of(128 * (m // 2), 128), 128)]
    tap_ref[...] = jnp.transpose(stacked([group[k : k + 1] for k in range(4)], (128, 128)))
    tap_cols = tap_ref[pl.ds(pl.multiple_of(64 * (m % 2), 64), 64), :]
    taps = [tap_cols[:, k : k + 1] for k in range(4)]

    def rows_of(d, lo, hi):
        for j in range(SEQ):
            ref = own_ref if j < 8 else oth_ref
            at = pl.multiple_of(16 * ab_ref[32 * j + d], 16)
            win_ref[WIN * j : WIN * j + WIN, :] = ref[j % 8, pl.ds(at, WIN), :]
        code = code_ref[pl.ds(d, 1), :][:, lo:hi]
        source = code >> 7
        j_of = (source >> 1) + 8 * ((source + c) & 1)
        key = j_of * WIN + ((code >> 2) & (WIN - 1))
        spread = one_hot(key, KEYS)
        return pick_quarter(dot(win_ref[...], spread, ((0,), (0,))), code & 3)

    first = 8 * c
    prev = rows_of(jnp.maximum(first - 1, 0), ROWS - 128, ROWS)
    prev = jnp.where(first > 0, prev, 0.0)

    for e in range(8):
        cur = rows_of(first + e, 0, ROWS)
        out_ref = out_a if e < 4 else out_b
        out_ref[:, ROWS * (e % 4) : ROWS * (e % 4) + ROWS] = conv_silu(cur, prev, taps).astype(BF)
        prev = cur[:, ROWS - 128 :]


def tile_at(ab_ref, c, s, d):
    j = (s >> 1) + 8 * ((s + c) % 2)
    return pl.multiple_of(16 * ab_ref[32 * j + d], 16)


def time_body(
    at_ref, ab_ref, bias_ref, rate_ref, skip_ref, code_ref, own_ref, oth_ref, conv_ref,
    table_ref, win_ref, col_ref, step_ref, tap_ref
):
    c, sq = at_ref[1], at_ref[2]
    head = sq // 2
    group = conv_ref[:, pl.ds(pl.multiple_of(128 * head, 128), 128)]
    tap_ref[...] = jnp.transpose(stacked([group[k : k + 1] for k in range(4)], (128, 128)))
    table_ref[64:, :128] = tap_ref[pl.ds(pl.multiple_of(64 * (sq % 2), 64), 64), :]
    table_ref[0:SEQ, :] = code_ref[...].astype(F32)
    table_ref[48:64, :] = jnp.full((16, ROWS), skip_ref[head], F32)
    for core, ref in enumerate((own_ref, oth_ref)):
        blocks = []
        for z in range(8):
            side = ref[z, QUAD:SLOT, :].astype(F32)
            side = pltpu.roll(side, 10, 0)[0:8]
            blocks += [side[:, :128], side[:, 128:]]
        turned = jnp.transpose(jnp.concatenate(blocks, axis=0))
        for z in range(8):
            own = turned if z == 0 else pltpu.roll(turned, 128 - 16 * z, 1)
            col_ref[8 * core + z] = own.astype(BF)

    def gather(d, carry):
        for j in range(SEQ):
            at = pl.multiple_of(16 * ab_ref[32 * j + d], 16)
            win_ref[WIN * j : WIN * j + WIN, :] = col_ref[j, pl.ds(at, WIN), :]
        code = code_ref[pl.ds(d, 1), :]
        source = code >> 7
        j_of = (source >> 1) + 8 * ((source + c) & 1)
        spread = one_hot(j_of * WIN + ((code >> 2) & (WIN - 1)), KEYS)
        quarter = code & 3
        parts = dot(win_ref[...], spread, ((0,), (0,)))
        step = jnp.zeros((1, ROWS), F32)
        for q in range(4):
            row = (q >> 1) + 8 * (q & 1)
            value = parts[row : row + 1] + parts[row + 2 : row + 3] + parts[row + 4 : row + 5]
            step = step + jnp.where(quarter == q, value, 0.0)
        step_ref[pl.ds(d, 1), :] = step
        return carry

    lax.fori_loop(0, SEQ, gather, 0, unroll=4)

    raw = step_ref[...] + bias_ref[head]
    size = jnp.maximum(raw, 0.0) + jnp.log1p(jnp.exp(-jnp.abs(raw)))
    table_ref[SEQ : 2 * SEQ, :] = size
    rate = jnp.exp(jnp.full((1, ROWS), rate_ref[head], F32))
    cum = -rate * size
    lane = iota((SEQ, ROWS), 1) & (BLOCK - 1)
    shift = 1
    while shift < BLOCK:
        cum = cum + jnp.where(lane >= shift, pltpu.roll(cum, shift, 1), 0.0)
        shift *= 2
    table_ref[2 * SEQ : 3 * SEQ, :] = cum


def gate_body(lat_ref, w_ref, out_ref):
    out_ref[...] = silu(dot(lat_ref[...], w_ref[...])).astype(BF)


def spread_of(table_ref, d):
    code = table_ref[pl.ds(d, 1), :].astype(I32)
    return one_hot((code >> 7) * WIN + ((code >> 2) & (WIN - 1)), KEYS), code & 3


def place_half(first, prev, at_ref, ab_ref, table_ref, x_ref, xact_ref, win_ref):
    c = at_ref[1]
    taps = [table_ref[64:, k : k + 1] for k in range(4)]

    def gather(e, prev):
        d = first + e
        for s in range(SEQ):
            at = tile_at(ab_ref, c, s, d)
            win_ref[WIN * s : WIN * s + WIN, :] = x_ref[s, pl.ds(at, WIN), :]
        spread, quarter = spread_of(table_ref, d)
        cur = pick_quarter(dot(win_ref[...], spread, ((0,), (0,))), quarter)
        act = conv_silu(cur, prev, taps)
        xact_ref[:, pl.ds(pl.multiple_of(ROWS * e, ROWS), ROWS)] = act.astype(BF)
        return cur[:, ROWS - 128 :]

    return lax.fori_loop(0, SEQ // 2, gather, prev, unroll=4)


def place_first(at_ref, ab_ref, table_ref, x_ref, xact_ref, last_ref, win_ref):
    prev = jnp.zeros((CH, 128), F32)
    last_ref[...] = place_half(0, prev, at_ref, ab_ref, table_ref, x_ref, xact_ref, win_ref)


def place_second(at_ref, ab_ref, table_ref, x_ref, last_ref, xact_ref, win_ref):
    place_half(8, last_ref[...], at_ref, ab_ref, table_ref, x_ref, xact_ref, win_ref)


def scan_body(at_ref, ab_ref, table_ref, xact_a, xact_b, *refs):
    owns, oths = refs[:8], refs[8:16]
    out_ref, bc_ref, sem_ref = refs[16:]
    m, c = at_ref[0], at_ref[1]
    copies = []
    for index in range(8):
        rows = pl.ds(pl.multiple_of(CH * ((m - index // 2 + 4) % 4), CH), CH)
        cols = pl.ds(4 * ROWS * (index % 2), 4 * ROWS)
        for side, ref in enumerate((owns[index], oths[index])):
            half = c if side == 0 else 1 - c
            copies.append(
                pltpu.make_async_copy(ref, bc_ref.at[half, rows, cols], sem_ref.at[index, side])
            )
    for copy in copies:
        copy.start()
    out_ref[...] = jnp.zeros_like(out_ref)
    skip = table_ref[48:49, :BLOCK]
    causal = iota((BLOCK, BLOCK), 0) <= iota((BLOCK, BLOCK), 1)
    def scan(half, e, state):
        d = 8 * half + e
        cols = pl.ds(pl.multiple_of(ROWS * e, ROWS), ROWS)
        x_all = (xact_b if half else xact_a)[:, cols].astype(F32)
        bc = bc_ref[half, :, cols]
        size_all = table_ref[pl.ds(SEQ + d, 1), :]
        cum_all = table_ref[pl.ds(2 * SEQ + d, 1), :]
        ys = []
        for k in range(ROWS // BLOCK):
            at = slice(BLOCK * k, BLOCK * k + BLOCK)
            x, b, cc = x_all[:, at], bc[:BC, at], bc[BC:, at]
            cum_row, size = cum_all[:, at], size_all[:, at]
            scores = dot(b, cc, ((0,), (0,)))
            col = column(cum_row)
            gap = cum_row - jnp.concatenate([col] * (BLOCK // 128), axis=1)
            weight = (scores * jnp.exp(jnp.where(causal, gap, -1e30))).astype(BF)
            y = dot((x * size).astype(BF), weight)
            y = y + dot(state.astype(BF), cc) * jnp.exp(cum_row) + skip * x
            ys.append(y)
            total = cum_row[:, BLOCK - 1 :]
            scaled = (x * (jnp.exp(total - cum_row) * size)).astype(BF)
            state = jnp.exp(total) * state + dot(scaled, b, ((1,), (1,)))
        y_all = jnp.concatenate(ys, axis=1)
        spread, quarter = spread_of(table_ref, d)
        apart = jnp.concatenate(
            [jnp.where(quarter == q, y_all, 0.0).astype(BF) for q in range(4)], axis=0
        )
        back = dot(spread, apart, ((1,), (1,)))
        for s in range(SEQ):
            at = pl.ds(tile_at(ab_ref, c, s, d), WIN)
            out_ref[s, at, :] = out_ref[s, at, :] + back[WIN * s : WIN * s + WIN].astype(BF)
        return state

    state = jnp.zeros((CH, BC), F32)
    for half in range(2):
        for index in range(8):
            rows = pl.ds(pl.multiple_of(CH * ((m - index // 2 + 4) % 4), CH), CH)
            cols = pl.ds(4 * ROWS * (index % 2), 4 * ROWS)
            sem = sem_ref.at[index, c if half == 0 else 1 - c]
            pltpu.make_async_copy(owns[index], bc_ref.at[half, rows, cols], sem).wait()
        state = lax.fori_loop(0, 8, lambda e, state, half=half: scan(half, e, state), state, unroll=8)


def final_body(inv_ref, y_ref, gate_hbm, gain_ref, out_ref, pick_ref, gate_ref, sem_ref):
    h = pl.program_id(0)

    def gate_copy(n):
        part = pl.ds(pl.multiple_of(256 * n, 256), 256)
        return pltpu.make_async_copy(gate_hbm.at[:, part], gate_ref.at[n], sem_ref.at[n])

    @pl.when(h == 0)
    def _():
        for n in range(gate_ref.shape[0]):
            gate_copy(n).start()
        inv = inv_ref[...].astype(F32)
        place = column(sorted_place(inv, column(inv)))
        lane = iota((ROWS, 128), 1)
        for g in range(4):
            hit = place == (lane + 128 * g).astype(F32)
            pick_ref[:, 128 * g : 128 * g + 128] = hit.astype(F32).astype(BF)

    low = iota((QUAD, 128), 1) < 64
    heads = []
    for n in range(2):
        rows = []
        for q in range(4):
            at = slice(128 * (q // 2), 128 * (q // 2) + 128)
            even = y_ref[4 * h + 2 * n, :, at].astype(F32)
            odd = y_ref[4 * h + 2 * n + 1, :, at].astype(F32)
            if q % 2 == 0:
                rows.append(jnp.where(low, even, pltpu.roll(odd, 64, 1)))
            else:
                rows.append(jnp.where(low, pltpu.roll(even, 64, 1), odd))
        heads.append(jnp.concatenate(rows, axis=0).astype(BF))
    y = dot(pick_ref[...], jnp.concatenate(heads, axis=1))
    gate_copy(h).wait()
    for n in range(2):
        at = slice(128 * n, 128 * n + 128)
        gated = y[:, at] * gate_ref[h, :, at].astype(F32)
        mean = jnp.mean(gated * gated, axis=1, keepdims=True)
        out_ref[:, at] = (gated * lax.rsqrt(mean + 1e-5) * gain_ref[:, at]).astype(BF)


def vmem(*_):
    return pl.BlockSpec(memory_space=pltpu.VMEM)


def hbm(*_):
    return pl.BlockSpec(memory_space=pl.ANY)


def smem(*_):
    return pl.BlockSpec(memory_space=pltpu.SMEM)


def params(mib):
    return pltpu.CompilerParams(vmem_limit_bytes=mib * MIB)


def cost(flops, data, exps=0):
    return pl.CostEstimate(flops=flops, bytes_accessed=data, transcendentals=exps)


def run_time(*args):
    return pl.pallas_call(
        time_body,
        out_shape=jax.ShapeDtypeStruct((128, ROWS), F32),
        in_specs=[smem()] * 5 + [vmem()] * 4,
        out_specs=vmem(),
        scratch_shapes=[
            pltpu.VMEM((KEYS, 128), BF),
            pltpu.VMEM((SEQ, 128, 128), BF),
            pltpu.VMEM((SEQ, ROWS), F32),
            pltpu.VMEM((128, 128), F32),
        ],
        compiler_params=params(8),
        cost_estimate=cost(2 << 30, 2 << 20),
        name="time",
    )(*args)


def run_place(kernel, outs, *args):
    return pl.pallas_call(
        kernel,
        out_shape=outs,
        in_specs=[smem()] * 2 + [vmem()] * (len(args) - 2),
        out_specs=tuple(vmem() for _ in outs),
        scratch_shapes=[pltpu.VMEM((KEYS, 256), BF)],
        compiler_params=params(24),
        cost_estimate=cost(2 << 30, 2 << 20),
        name="place",
    )(*args)


def run_scan(*args):
    return pl.pallas_call(
        scan_body,
        out_shape=jax.ShapeDtypeStruct((SEQ, QUAD, 256), BF),
        in_specs=[smem()] * 2 + [vmem()] * 3 + [hbm()] * 16,
        out_specs=vmem(),
        scratch_shapes=[
            pltpu.VMEM((2, 256, 8 * ROWS), BF),
            pltpu.SemaphoreType.DMA((8, 2)),
        ],
        compiler_params=params(24),
        cost_estimate=cost(8 << 30, 8 << 20),
        name="scan",
    )(*args)


def run_front(*args):
    return pl.pallas_call(
        front_body,
        out_shape=jax.ShapeDtypeStruct((8, SLOT, 256), BF),
        in_specs=[hbm(), hbm(), hbm(), hbm(), vmem()],
        out_specs=vmem(),
        scratch_shapes=[
            pltpu.VMEM((1, ROWS), I32),
            pltpu.VMEM((1, ROWS), I32),
            pltpu.VMEM(args[2].shape, BF),
            pltpu.VMEM(args[3].shape, BF),
            pltpu.SemaphoreType.DMA((10,)),
        ],
        compiler_params=params(60),
        cost_estimate=cost(1 << 30, 4 << 20),
        name="front",
    )(*args)


def body(
    latent,
    order,
    inverse,
    w_gate,
    w_value,
    w_input_output,
    w_step,
    conv_value,
    conv_input_output,
    step_bias,
    log_rate,
    skip_gain,
    norm_gain,
):
    m, sq = lax.axis_index("mp"), lax.axis_index("seq")
    at = jnp.stack([m, sq % 2, sq, m]).astype(I32)
    inv = inverse.reshape(1, ROWS)
    pairs = [(i, i ^ 1) for i in range(SEQ)]
    lines = [[2 * i + core for i in range(SEQ // 2)] for core in range(2)]

    bc_slots = run_front(inv, order.reshape(1, ROWS), latent, w_input_output, w_step.T)
    own = lax.all_to_all(bc_slots, "seq", 0, 0, axis_index_groups=lines, tiled=True)

    x_slots = pl.pallas_call(
        value_body,
        grid=(4,),
        out_shape=jax.ShapeDtypeStruct((SEQ, QUAD, 256), BF),
        in_specs=[
            pl.BlockSpec((1, ROWS), lambda n: (0, 0)),
            pl.BlockSpec((ROWS, latent.shape[1]), lambda n: (0, 0)),
            pl.BlockSpec((latent.shape[1], 256), lambda n: (0, n)),
        ],
        out_specs=pl.BlockSpec((4, QUAD, 256), lambda n: (n, 0, 0)),
        scratch_shapes=[pltpu.VMEM((ROWS, ROWS), BF)],
        compiler_params=params(24),
        cost_estimate=cost(3 << 30, 8 << 20),
        name="value",
    )(inv, latent, w_value)
    gate = pl.pallas_call(
        gate_body,
        grid=(4,),
        out_shape=jax.ShapeDtypeStruct((ROWS, w_gate.shape[1]), BF),
        in_specs=[
            pl.BlockSpec((ROWS, latent.shape[1]), lambda n: (0, 0)),
            pl.BlockSpec((latent.shape[1], 256), lambda n: (0, n)),
        ],
        out_specs=pl.BlockSpec((ROWS, 256), lambda n: (0, n)),
        compiler_params=params(24),
        cost_estimate=cost(2 << 30, 8 << 20),
        name="gate",
    )(latent, w_gate)

    x_slots, own = lax.optimization_barrier((x_slots, own))
    oth = lax.ppermute(own, "seq", pairs)
    x_all = lax.all_to_all(x_slots, "seq", 0, 0, tiled=True)

    side = jnp.concatenate([own[:, QUAD + 4 : QUAD + 6, :16], oth[:, QUAD + 4 : QUAD + 6, :16]], 0)
    ab = side.astype(I32).reshape(-1)
    half = jax.ShapeDtypeStruct((CH, 4 * ROWS), BF)
    bc_a, bc_b, code = pl.pallas_call(
        bc_body,
        out_shape=(half, half, jax.ShapeDtypeStruct((SEQ, ROWS), I32)),
        in_specs=[smem(), smem(), vmem(), vmem(), vmem()],
        out_specs=(vmem(), vmem(), vmem()),
        scratch_shapes=[pltpu.VMEM((KEYS, 256), BF), pltpu.VMEM((128, 128), F32)],
        compiler_params=params(8),
        cost_estimate=cost(1 << 30, 2 << 20),
        name="bc",
    )(at, ab, own, oth, conv_input_output)
    up = [(i, (i + 1) % 4) for i in range(4)]
    down = [(i, (i - 1) % 4) for i in range(4)]
    one_a, three_b = lax.ppermute(bc_a, "mp", up), lax.ppermute(bc_b, "mp", down)
    one_b, three_a = lax.ppermute(bc_b, "mp", up), lax.ppermute(bc_a, "mp", down)
    table = run_time(at, ab, step_bias, log_rate, skip_gain, code, own, oth, conv_value)
    one_a, three_b, table = lax.optimization_barrier((one_a, three_b, table))
    two_a, two_b = lax.ppermute(one_a, "mp", up), lax.ppermute(three_b, "mp", down)
    owns = [bc_a, bc_b, one_a, one_b, two_a, two_b, three_a, three_b]
    part = jax.ShapeDtypeStruct((CH, 8 * ROWS), BF)
    last = jax.ShapeDtypeStruct((CH, 128), F32)
    xact_a, last = run_place(place_first, (part, last), at, ab, table, x_all)
    owns, xact_a = lax.optimization_barrier((owns, xact_a))
    oths = [lax.ppermute(v, "seq", pairs) for v in owns]
    (xact_b,) = run_place(place_second, (part,), at, ab, table, x_all, last)
    y_slots = run_scan(at, ab, table, xact_a, xact_b, *owns, *oths)
    y_all = lax.all_to_all(y_slots, "seq", 0, 0, tiled=True)

    heads = step_bias.shape[0]
    return pl.pallas_call(
        final_body,
        grid=(heads // 2,),
        out_shape=jax.ShapeDtypeStruct((ROWS, heads * 128), BF),
        in_specs=[
            pl.BlockSpec((1, ROWS), lambda h: (0, 0)),
            vmem(),
            hbm(),
            pl.BlockSpec((1, 256), lambda h: (0, h)),
        ],
        out_specs=pl.BlockSpec((ROWS, 256), lambda h: (0, h)),
        scratch_shapes=[
            pltpu.VMEM((ROWS, ROWS), BF),
            pltpu.VMEM((heads // 2, ROWS, 256), BF),
            pltpu.SemaphoreType.DMA((heads // 2,)),
        ],
        compiler_params=params(12),
        cost_estimate=cost(1 << 30, 3 << 20),
        name="final",
    )(inv, y_all, gate, norm_gain.reshape(1, -1))


def solution(mesh):
    return jax.shard_map(
        body,
        mesh=mesh,
        in_specs=(
            P(("batch", "seq"), None),
            P("seq"),
            P("seq"),
            P(None, "mp"),
            P(None, "mp"),
            P(),
            P(None, "mp"),
            P(None, "mp"),
            P(),
            P("mp"),
            P("mp"),
            P("mp"),
            P("mp"),
        ),
        out_specs=P(("batch", "seq"), "mp"),
        check_vma=False,
    )
```

```python
import jax
import jax.numpy as jnp
from jax import lax
from jax.experimental import pallas as pl
from jax.experimental.pallas import tpu as pltpu
from jax.sharding import PartitionSpec as P

F32, BF, I32 = jnp.float32, jnp.bfloat16, jnp.int32
ROWS = 512
SEQ = 16
QUAD = ROWS // 4
SLOT = QUAD + 16
WIN = 32
KEYS = SEQ * WIN
CH = 64
BLOCK = 256
BC = 128
MIB = 1 << 20


def iota(shape, dim):
    return lax.broadcasted_iota(I32, shape, dim)


def dot(a, b, dims=((1,), (0,))):
    return lax.dot_general(a, b, (dims, ((), ())), preferred_element_type=F32)


def column(row):
    return jnp.transpose(jnp.broadcast_to(row, (128, row.shape[1])))


def tiles(row):
    return [row[:, g : g + 128] for g in range(0, row.shape[1], 128)]


def sorted_place(inv, inv_col):
    rank = jnp.concatenate(
        [jnp.sum((inv_col < part).astype(F32), axis=0, keepdims=True) for part in tiles(inv)],
        axis=1,
    )
    packed = jnp.floor(rank * 0.25)
    return (rank - 4.0 * packed) * QUAD + packed


def one_hot(place, count):
    row = iota((count, place.shape[1]), 0).astype(jnp.int16)
    return jnp.where(row == place.astype(I32).astype(jnp.int16), BF(1), BF(0))


def stacked(rows, shape):
    place = iota(shape, 0)
    block = jnp.zeros(shape, F32)
    for index, row in enumerate(rows):
        block = jnp.where(place == index, row, block)
    return block


def side_by_side(low, high):
    first = iota((QUAD, 128), 1) < 64
    return [
        jnp.where(first, low[u : u + QUAD], high[u + QUAD : u + 2 * QUAD]) for u in (0, 2 * QUAD)
    ]


def front_body(
    inv_hbm,
    ord_hbm,
    lat_hbm,
    wio_hbm,
    ws_ref,
    out_ref,
    inv_ref,
    ord_ref,
    lat_ref,
    wio_ref,
    sem_ref,
):
    small = [
        pltpu.make_async_copy(inv_hbm, inv_ref, sem_ref.at[0]),
        pltpu.make_async_copy(ord_hbm, ord_ref, sem_ref.at[1]),
    ]
    large = []
    for k in range(4):
        part = pl.ds(512 * k, 512)
        large.append(
            (
                pltpu.make_async_copy(lat_hbm.at[:, part], lat_ref.at[:, part], sem_ref.at[2 + k]),
                pltpu.make_async_copy(wio_hbm.at[part], wio_ref.at[part], sem_ref.at[6 + k]),
            )
        )
    for copy in small:
        copy.start()
    for pair in large:
        for copy in pair:
            copy.start()
    for copy in small:
        copy.wait()
    inv = inv_ref[...].astype(F32)
    inv_col = column(inv)
    deal = one_hot(sorted_place(inv, inv_col), ROWS)
    source = (ord_ref[...] >> 9).astype(F32)
    source_col = column(source)
    earlier = [
        jnp.sum(
            jnp.where(
                (source_col == part) & (iota((ROWS, 128), 0) < iota((ROWS, 128), 1) + 128 * g),
                1.0,
                0.0,
            ),
            axis=0,
            keepdims=True,
        )
        for g, part in enumerate(tiles(source))
    ]
    bound = (iota((ROWS, 128), 1) * ROWS).astype(F32)
    start = jnp.sum((inv_col < bound).astype(F32), axis=0, keepdims=True)
    tile = jnp.minimum(jnp.floor(start * (1.0 / 64.0)), 6.0)
    offset = start - 64.0 * tile
    blank = jnp.zeros((1, 128), F32)
    rows = [
        source[:, :256],
        source[:, 256:],
        jnp.concatenate(earlier[:2], axis=1),
        jnp.concatenate(earlier[2:], axis=1),
        jnp.concatenate([tile, blank], axis=1),
        jnp.concatenate([offset, blank], axis=1),
    ]
    io = jnp.zeros((ROWS, 256), F32)
    rest = jnp.zeros((ROWS, 128), F32)
    ws = jnp.concatenate([ws_ref[...], jnp.zeros((120, ws_ref.shape[1]), BF)], axis=0)
    for k, pair in enumerate(large):
        for copy in pair:
            copy.wait()
        part = slice(512 * k, 512 * k + 512)
        io = io + dot(lat_ref[:, part], wio_ref[part, :])
        rest = rest + dot(lat_ref[:, part], ws[:, part], ((1,), (1,)))
    io = dot(deal, io.astype(BF))
    rest = jnp.transpose(rest)[:8]
    pieces = []
    for _ in range(3):
        piece = rest.astype(BF)
        pieces.append(piece.astype(F32))
        rest = rest - pieces[-1]
    pieces = jnp.concatenate(pieces + [rest], axis=0).astype(BF)
    dealt = dot(pieces, deal, ((1,), (1,)))
    steps = [dealt[8 * k : 8 * k + 8] for k in range(3)]
    m = lax.axis_index("mp")
    half = jnp.where(m >= 2, io[:, 128:], io[:, :128])
    turned = pltpu.roll(half, 64, 1)
    odd = m % 2 == 1
    packed = side_by_side(jnp.where(odd, turned, half), jnp.where(odd, half, turned))
    slot = jnp.concatenate(packed, axis=1).astype(BF)
    for head in range(out_ref.shape[0]):
        halves = []
        for step in steps:
            own = step[head : head + 1]
            halves += [own[:, :256], own[:, 256:]]
        out_ref[head, :QUAD, :] = slot
        out_ref[head, QUAD:, :] = stacked(rows + halves, (16, 256)).astype(BF)


def value_body(inv_ref, lat_ref, wv_ref, out_ref, deal_ref):
    @pl.when(pl.program_id(0) == 0)
    def _():
        inv = inv_ref[...].astype(F32)
        deal_ref[...] = one_hot(sorted_place(inv, column(inv)), ROWS)

    value = dot(lat_ref[...], wv_ref[...]).astype(BF)
    value = dot(deal_ref[...], value)
    for jj in range(4):
        group = value[:, 128 * (jj // 2) : 128 * (jj // 2) + 128]
        turned = pltpu.roll(group, 64, 1)
        packed = side_by_side(group, turned) if jj % 2 == 0 else side_by_side(turned, group)
        out_ref[jj] = jnp.concatenate(packed, axis=1).astype(BF)


def silu(x):
    half = 0.5 * x
    return half + half * jnp.tanh(half)


def conv_silu(cur, prev, taps):
    ext = jnp.concatenate([prev, cur], axis=1)
    total = cur * taps[3]
    for back in range(1, 4):
        total = total + pltpu.roll(ext, back, 1)[:, 128:] * taps[3 - back]
    return silu(total)


def pick_quarter(res, quarter):
    out = jnp.zeros((CH, res.shape[1]), F32)
    for q in range(4):
        out = out + jnp.where(quarter == q, res[CH * q : CH * q + CH], 0.0)
    return out


def code_body(at_ref, ab_ref, own_ref, oth_ref, code_ref):
    c = at_ref[1]
    for z in range(8):
        for ref, core in ((own_ref, c), (oth_ref, 1 - c)):
            d = 2 * z + core
            side = ref[z, QUAD:SLOT, :].astype(F32)
            source = jnp.concatenate([side[0:1], side[1:2]], axis=1).astype(I32)
            place = jnp.concatenate([side[2:3], side[3:4]], axis=1).astype(I32)
            for s in range(SEQ):
                j = (s >> 1) + 8 * ((s + c) % 2)
                place = place + jnp.where(source == s, ab_ref[32 * j + 16 + d], 0)
            code_ref[pl.ds(d, 1), :] = source * 128 + place


def bc_body(
    at_ref, ab_ref, own_ref, oth_ref, conv_ref, out_a, out_b, code_ref, win_ref, tap_ref
):
    code_body(at_ref, ab_ref, own_ref, oth_ref, code_ref)
    m, c = at_ref[0], at_ref[1]
    group = conv_ref[:, pl.ds(pl.multiple_of(128 * (m // 2), 128), 128)]
    tap_ref[...] = jnp.transpose(stacked([group[k : k + 1] for k in range(4)], (128, 128)))
    tap_cols = tap_ref[pl.ds(pl.multiple_of(64 * (m % 2), 64), 64), :]
    taps = [tap_cols[:, k : k + 1] for k in range(4)]

    def rows_of(d, lo, hi):
        for j in range(SEQ):
            ref = own_ref if j < 8 else oth_ref
            at = pl.multiple_of(16 * ab_ref[32 * j + d], 16)
            win_ref[WIN * j : WIN * j + WIN, :] = ref[j % 8, pl.ds(at, WIN), :]
        code = code_ref[pl.ds(d, 1), :][:, lo:hi]
        source = code >> 7
        j_of = (source >> 1) + 8 * ((source + c) & 1)
        key = j_of * WIN + ((code >> 2) & (WIN - 1))
        spread = one_hot(key, KEYS)
        return pick_quarter(dot(win_ref[...], spread, ((0,), (0,))), code & 3)

    first = 8 * c
    prev = rows_of(jnp.maximum(first - 1, 0), ROWS - 128, ROWS)
    prev = jnp.where(first > 0, prev, 0.0)

    for e in range(8):
        cur = rows_of(first + e, 0, ROWS)
        out_ref = out_a if e < 4 else out_b
        out_ref[:, ROWS * (e % 4) : ROWS * (e % 4) + ROWS] = conv_silu(cur, prev, taps).astype(BF)
        prev = cur[:, ROWS - 128 :]


def tile_at(ab_ref, c, s, d):
    j = (s >> 1) + 8 * ((s + c) % 2)
    return pl.multiple_of(16 * ab_ref[32 * j + d], 16)


def time_body(
    at_ref, ab_ref, bias_ref, rate_ref, skip_ref, code_ref, own_ref, oth_ref, conv_ref,
    table_ref, win_ref, col_ref, step_ref, tap_ref
):
    c, sq = at_ref[1], at_ref[2]
    head = sq // 2
    group = conv_ref[:, pl.ds(pl.multiple_of(128 * head, 128), 128)]
    tap_ref[...] = jnp.transpose(stacked([group[k : k + 1] for k in range(4)], (128, 128)))
    table_ref[64:, :128] = tap_ref[pl.ds(pl.multiple_of(64 * (sq % 2), 64), 64), :]
    table_ref[0:SEQ, :] = code_ref[...].astype(F32)
    table_ref[48:64, :] = jnp.full((16, ROWS), skip_ref[head], F32)
    for core, ref in enumerate((own_ref, oth_ref)):
        blocks = []
        for z in range(8):
            side = ref[z, QUAD:SLOT, :].astype(F32)
            side = pltpu.roll(side, 10, 0)[0:8]
            blocks += [side[:, :128], side[:, 128:]]
        turned = jnp.transpose(jnp.concatenate(blocks, axis=0))
        for z in range(8):
            own = turned if z == 0 else pltpu.roll(turned, 128 - 16 * z, 1)
            col_ref[8 * core + z] = own.astype(BF)

    def gather(d, carry):
        for j in range(SEQ):
            at = pl.multiple_of(16 * ab_ref[32 * j + d], 16)
            win_ref[WIN * j : WIN * j + WIN, :] = col_ref[j, pl.ds(at, WIN), :]
        code = code_ref[pl.ds(d, 1), :]
        source = code >> 7
        j_of = (source >> 1) + 8 * ((source + c) & 1)
        spread = one_hot(j_of * WIN + ((code >> 2) & (WIN - 1)), KEYS)
        quarter = code & 3
        parts = dot(win_ref[...], spread, ((0,), (0,)))
        step = jnp.zeros((1, ROWS), F32)
        for q in range(4):
            row = (q >> 1) + 8 * (q & 1)
            value = parts[row : row + 1] + parts[row + 2 : row + 3] + parts[row + 4 : row + 5]
            step = step + jnp.where(quarter == q, value, 0.0)
        step_ref[pl.ds(d, 1), :] = step
        return carry

    lax.fori_loop(0, SEQ, gather, 0, unroll=4)

    raw = step_ref[...] + bias_ref[head]
    size = jnp.maximum(raw, 0.0) + jnp.log1p(jnp.exp(-jnp.abs(raw)))
    table_ref[SEQ : 2 * SEQ, :] = size
    rate = jnp.exp(jnp.full((1, ROWS), rate_ref[head], F32))
    cum = -rate * size
    lane = iota((SEQ, ROWS), 1) & (BLOCK - 1)
    shift = 1
    while shift < BLOCK:
        cum = cum + jnp.where(lane >= shift, pltpu.roll(cum, shift, 1), 0.0)
        shift *= 2
    table_ref[2 * SEQ : 3 * SEQ, :] = cum


def gate_body(lat_ref, w_ref, out_ref):
    out_ref[...] = silu(dot(lat_ref[...], w_ref[...])).astype(BF)


def spread_of(table_ref, d):
    code = table_ref[pl.ds(d, 1), :].astype(I32)
    return one_hot((code >> 7) * WIN + ((code >> 2) & (WIN - 1)), KEYS), code & 3


def place_half(first, prev, at_ref, ab_ref, table_ref, x_ref, xact_ref, win_ref):
    c = at_ref[1]
    taps = [table_ref[64:, k : k + 1] for k in range(4)]

    def gather(e, prev):
        d = first + e
        for s in range(SEQ):
            at = tile_at(ab_ref, c, s, d)
            win_ref[WIN * s : WIN * s + WIN, :] = x_ref[s, pl.ds(at, WIN), :]
        spread, quarter = spread_of(table_ref, d)
        cur = pick_quarter(dot(win_ref[...], spread, ((0,), (0,))), quarter)
        act = conv_silu(cur, prev, taps)
        xact_ref[:, pl.ds(pl.multiple_of(ROWS * e, ROWS), ROWS)] = act.astype(BF)
        return cur[:, ROWS - 128 :]

    return lax.fori_loop(0, SEQ // 2, gather, prev, unroll=4)


def place_first(at_ref, ab_ref, table_ref, x_ref, *refs):
    parts, (xact_ref, last_ref, bundle_ref, win_ref, sem_ref) = refs[:4], refs[4:]
    copies = [
        pltpu.make_async_copy(part, bundle_ref.at[k], sem_ref.at[k]) for k, part in enumerate(parts)
    ]
    for copy in copies:
        copy.start()
    prev = jnp.zeros((CH, 128), F32)
    last_ref[...] = place_half(0, prev, at_ref, ab_ref, table_ref, x_ref, xact_ref, win_ref)
    for copy in copies:
        copy.wait()


def place_second(at_ref, ab_ref, table_ref, x_ref, last_ref, xact_ref, win_ref):
    place_half(8, last_ref[...], at_ref, ab_ref, table_ref, x_ref, xact_ref, win_ref)


def scan_body(at_ref, ab_ref, table_ref, xact_a, xact_b, *refs):
    owns, bundle, late = refs[:8], refs[8], refs[9:13]
    out_ref, bc_ref, sem_ref = refs[13:]
    oths = [bundle.at[0], bundle.at[1], bundle.at[2], *late, bundle.at[3]]
    m, c = at_ref[0], at_ref[1]
    copies = []
    for index in range(8):
        rows = pl.ds(pl.multiple_of(CH * ((m - index // 2 + 4) % 4), CH), CH)
        cols = pl.ds(4 * ROWS * (index % 2), 4 * ROWS)
        for side, ref in enumerate((owns[index], oths[index])):
            half = c if side == 0 else 1 - c
            copies.append(
                pltpu.make_async_copy(ref, bc_ref.at[half, rows, cols], sem_ref.at[index, side])
            )
    for copy in copies:
        copy.start()
    out_ref[...] = jnp.zeros_like(out_ref)
    skip = table_ref[48:49, :BLOCK]
    causal = iota((BLOCK, BLOCK), 0) <= iota((BLOCK, BLOCK), 1)
    def scan(half, e, state):
        d = 8 * half + e
        cols = pl.ds(pl.multiple_of(ROWS * e, ROWS), ROWS)
        x_all = (xact_b if half else xact_a)[:, cols].astype(F32)
        bc = bc_ref[half, :, cols]
        size_all = table_ref[pl.ds(SEQ + d, 1), :]
        cum_all = table_ref[pl.ds(2 * SEQ + d, 1), :]
        ys = []
        for k in range(ROWS // BLOCK):
            at = slice(BLOCK * k, BLOCK * k + BLOCK)
            x, b, cc = x_all[:, at], bc[:BC, at], bc[BC:, at]
            cum_row, size = cum_all[:, at], size_all[:, at]
            scores = dot(b, cc, ((0,), (0,)))
            col = column(cum_row)
            gap = cum_row - jnp.concatenate([col] * (BLOCK // 128), axis=1)
            weight = (scores * jnp.exp(jnp.where(causal, gap, -1e30))).astype(BF)
            y = dot((x * size).astype(BF), weight)
            y = y + dot(state.astype(BF), cc) * jnp.exp(cum_row) + skip * x
            ys.append(y)
            total = cum_row[:, BLOCK - 1 :]
            scaled = (x * (jnp.exp(total - cum_row) * size)).astype(BF)
            state = jnp.exp(total) * state + dot(scaled, b, ((1,), (1,)))
        y_all = jnp.concatenate(ys, axis=1)
        spread, quarter = spread_of(table_ref, d)
        apart = jnp.concatenate(
            [jnp.where(quarter == q, y_all, 0.0).astype(BF) for q in range(4)], axis=0
        )
        back = dot(spread, apart, ((1,), (1,)))
        for s in range(SEQ):
            at = pl.ds(tile_at(ab_ref, c, s, d), WIN)
            out_ref[s, at, :] = out_ref[s, at, :] + back[WIN * s : WIN * s + WIN].astype(BF)
        return state

    state = jnp.zeros((CH, BC), F32)
    for half in range(2):
        for index in range(8):
            rows = pl.ds(pl.multiple_of(CH * ((m - index // 2 + 4) % 4), CH), CH)
            cols = pl.ds(4 * ROWS * (index % 2), 4 * ROWS)
            sem = sem_ref.at[index, c if half == 0 else 1 - c]
            pltpu.make_async_copy(owns[index], bc_ref.at[half, rows, cols], sem).wait()
        state = lax.fori_loop(0, 8, lambda e, state, half=half: scan(half, e, state), state, unroll=8)


def final_body(inv_ref, y_ref, gate_hbm, gain_ref, out_ref, pick_ref, gate_ref, sem_ref):
    h = pl.program_id(0)

    def gate_copy(n):
        part = pl.ds(pl.multiple_of(512 * n, 512), 512)
        return pltpu.make_async_copy(gate_hbm.at[:, part], gate_ref.at[n], sem_ref.at[n])

    @pl.when(h == 0)
    def _():
        for n in range(gate_ref.shape[0]):
            gate_copy(n).start()
        inv = inv_ref[...].astype(F32)
        place = column(sorted_place(inv, column(inv)))
        lane = iota((ROWS, 128), 1)
        for g in range(4):
            hit = place == (lane + 128 * g).astype(F32)
            pick_ref[:, 128 * g : 128 * g + 128] = hit.astype(F32).astype(BF)

    low = iota((QUAD, 128), 1) < 64
    heads = []
    for n in range(4):
        rows = []
        for q in range(4):
            at = slice(128 * (q // 2), 128 * (q // 2) + 128)
            even = y_ref[8 * h + 2 * n, :, at].astype(F32)
            odd = y_ref[8 * h + 2 * n + 1, :, at].astype(F32)
            if q % 2 == 0:
                rows.append(jnp.where(low, even, pltpu.roll(odd, 64, 1)))
            else:
                rows.append(jnp.where(low, pltpu.roll(even, 64, 1), odd))
        heads.append(jnp.concatenate(rows, axis=0).astype(BF))
    y = dot(pick_ref[...], jnp.concatenate(heads, axis=1))
    gate_copy(h).wait()
    for n in range(4):
        at = slice(128 * n, 128 * n + 128)
        gated = y[:, at] * gate_ref[h, :, at].astype(F32)
        mean = jnp.mean(gated * gated, axis=1, keepdims=True)
        out_ref[:, at] = (gated * lax.rsqrt(mean + 1e-5) * gain_ref[:, at]).astype(BF)


def vmem(*_):
    return pl.BlockSpec(memory_space=pltpu.VMEM)


def hbm(*_):
    return pl.BlockSpec(memory_space=pl.ANY)


def smem(*_):
    return pl.BlockSpec(memory_space=pltpu.SMEM)


def params(mib):
    return pltpu.CompilerParams(vmem_limit_bytes=mib * MIB)


def cost(flops, data, exps=0):
    return pl.CostEstimate(flops=flops, bytes_accessed=data, transcendentals=exps)


def run_time(*args):
    return pl.pallas_call(
        time_body,
        out_shape=jax.ShapeDtypeStruct((128, ROWS), F32),
        in_specs=[smem()] * 5 + [vmem()] * 4,
        out_specs=vmem(),
        scratch_shapes=[
            pltpu.VMEM((KEYS, 128), BF),
            pltpu.VMEM((SEQ, 128, 128), BF),
            pltpu.VMEM((SEQ, ROWS), F32),
            pltpu.VMEM((128, 128), F32),
        ],
        compiler_params=params(8),
        cost_estimate=cost(2 << 30, 2 << 20),
        name="time",
    )(*args)


def run_place(kernel, outs, args, parts=()):
    sems = [pltpu.SemaphoreType.DMA((len(parts),))] if parts else []
    return pl.pallas_call(
        kernel,
        out_shape=outs,
        in_specs=[smem()] * 2 + [vmem()] * (len(args) - 2) + [hbm()] * len(parts),
        out_specs=tuple(vmem() for _ in outs),
        scratch_shapes=[pltpu.VMEM((KEYS, 256), BF), *sems],
        compiler_params=params(24),
        cost_estimate=cost(2 << 30, 2 << 20),
        name="place",
    )(*args, *parts)


def run_scan(*args):
    return pl.pallas_call(
        scan_body,
        out_shape=jax.ShapeDtypeStruct((SEQ, QUAD, 256), BF),
        in_specs=[smem()] * 2 + [vmem()] * 3 + [hbm()] * 13,
        out_specs=vmem(),
        scratch_shapes=[
            pltpu.VMEM((2, 256, 8 * ROWS), BF),
            pltpu.SemaphoreType.DMA((8, 2)),
        ],
        compiler_params=params(24),
        cost_estimate=cost(8 << 30, 8 << 20),
        name="scan",
    )(*args)


def run_front(*args):
    return pl.pallas_call(
        front_body,
        out_shape=jax.ShapeDtypeStruct((8, SLOT, 256), BF),
        in_specs=[hbm(), hbm(), hbm(), hbm(), vmem()],
        out_specs=vmem(),
        scratch_shapes=[
            pltpu.VMEM((1, ROWS), I32),
            pltpu.VMEM((1, ROWS), I32),
            pltpu.VMEM(args[2].shape, BF),
            pltpu.VMEM(args[3].shape, BF),
            pltpu.SemaphoreType.DMA((10,)),
        ],
        compiler_params=params(60),
        cost_estimate=cost(1 << 30, 4 << 20),
        name="front",
    )(*args)


def run_final(*args):
    heads = args[1].shape[0] // 2
    return pl.pallas_call(
        final_body,
        grid=(heads // 4,),
        out_shape=jax.ShapeDtypeStruct((ROWS, heads * 128), BF),
        in_specs=[
            pl.BlockSpec((1, ROWS), lambda h: (0, 0)),
            vmem(),
            hbm(),
            pl.BlockSpec((1, 512), lambda h: (0, h)),
        ],
        out_specs=pl.BlockSpec((ROWS, 512), lambda h: (0, h)),
        scratch_shapes=[
            pltpu.VMEM((ROWS, ROWS), BF),
            pltpu.VMEM((heads // 4, ROWS, 512), BF),
            pltpu.SemaphoreType.DMA((heads // 4,)),
        ],
        compiler_params=params(12),
        cost_estimate=cost(1 << 30, 3 << 20),
        name="final",
    )(*args)


def body(
    latent,
    order,
    inverse,
    w_gate,
    w_value,
    w_input_output,
    w_step,
    conv_value,
    conv_input_output,
    step_bias,
    log_rate,
    skip_gain,
    norm_gain,
):
    m, sq = lax.axis_index("mp"), lax.axis_index("seq")
    at = jnp.stack([m, sq % 2, sq, m]).astype(I32)
    inv = inverse.reshape(1, ROWS)
    pairs = [(i, i ^ 1) for i in range(SEQ)]
    lines = [[2 * i + core for i in range(SEQ // 2)] for core in range(2)]

    bc_slots = run_front(inv, order.reshape(1, ROWS), latent, w_input_output, w_step.T)
    own = lax.all_to_all(bc_slots, "seq", 0, 0, axis_index_groups=lines, tiled=True)

    x_slots = pl.pallas_call(
        value_body,
        grid=(4,),
        out_shape=jax.ShapeDtypeStruct((SEQ, QUAD, 256), BF),
        in_specs=[
            pl.BlockSpec((1, ROWS), lambda n: (0, 0)),
            pl.BlockSpec((ROWS, latent.shape[1]), lambda n: (0, 0)),
            pl.BlockSpec((latent.shape[1], 256), lambda n: (0, n)),
        ],
        out_specs=pl.BlockSpec((4, QUAD, 256), lambda n: (n, 0, 0)),
        scratch_shapes=[pltpu.VMEM((ROWS, ROWS), BF)],
        compiler_params=params(24),
        cost_estimate=cost(3 << 30, 8 << 20),
        name="value",
    )(inv, latent, w_value)
    gate = pl.pallas_call(
        gate_body,
        grid=(4,),
        out_shape=jax.ShapeDtypeStruct((ROWS, w_gate.shape[1]), BF),
        in_specs=[
            pl.BlockSpec((ROWS, latent.shape[1]), lambda n: (0, 0)),
            pl.BlockSpec((latent.shape[1], 256), lambda n: (0, n)),
        ],
        out_specs=pl.BlockSpec((ROWS, 256), lambda n: (0, n)),
        compiler_params=params(24),
        cost_estimate=cost(2 << 30, 8 << 20),
        name="gate",
    )(latent, w_gate)

    x_slots, own = lax.optimization_barrier((x_slots, own))
    oth = lax.ppermute(own, "seq", pairs)
    x_all = lax.all_to_all(x_slots, "seq", 0, 0, tiled=True)

    side = jnp.concatenate([own[:, QUAD + 4 : QUAD + 6, :16], oth[:, QUAD + 4 : QUAD + 6, :16]], 0)
    ab = side.astype(I32).reshape(-1)
    half = jax.ShapeDtypeStruct((CH, 4 * ROWS), BF)
    bc_a, bc_b, code = pl.pallas_call(
        bc_body,
        out_shape=(half, half, jax.ShapeDtypeStruct((SEQ, ROWS), I32)),
        in_specs=[smem(), smem(), vmem(), vmem(), vmem()],
        out_specs=(vmem(), vmem(), vmem()),
        scratch_shapes=[pltpu.VMEM((KEYS, 256), BF), pltpu.VMEM((128, 128), F32)],
        compiler_params=params(8),
        cost_estimate=cost(1 << 30, 2 << 20),
        name="bc",
    )(at, ab, own, oth, conv_input_output)
    up = [(i, (i + 1) % 4) for i in range(4)]
    down = [(i, (i - 1) % 4) for i in range(4)]
    one_a, three_b = lax.ppermute(bc_a, "mp", up), lax.ppermute(bc_b, "mp", down)
    one_b, three_a = lax.ppermute(bc_b, "mp", up), lax.ppermute(bc_a, "mp", down)
    table = run_time(at, ab, step_bias, log_rate, skip_gain, code, own, oth, conv_value)
    one_a, three_b, table = lax.optimization_barrier((one_a, three_b, table))
    two_a, two_b = lax.ppermute(one_a, "mp", up), lax.ppermute(three_b, "mp", down)
    owns = [bc_a, bc_b, one_a, one_b, two_a, two_b, three_a, three_b]
    part = jax.ShapeDtypeStruct((CH, 8 * ROWS), BF)
    last = jax.ShapeDtypeStruct((CH, 128), F32)
    sheaf = jax.ShapeDtypeStruct((4, CH, 4 * ROWS), BF)
    xact_a, last, bundle = run_place(
        place_first, (part, last, sheaf), (at, ab, table, x_all), (bc_a, bc_b, one_a, three_b)
    )
    late, bundle, xact_a = lax.optimization_barrier((owns[3:7], bundle, xact_a))
    owns = [*owns[:3], *late, owns[7]]
    oths = [lax.ppermute(v, "seq", pairs) for v in (bundle, *late)]
    (xact_b,) = run_place(place_second, (part,), (at, ab, table, x_all, last))
    y_slots = run_scan(at, ab, table, xact_a, xact_b, *owns, *oths)
    y_all = lax.all_to_all(y_slots, "seq", 0, 0, tiled=True)

    return run_final(inv, y_all, gate, norm_gain.reshape(1, -1))


def solution(mesh):
    return jax.shard_map(
        body,
        mesh=mesh,
        in_specs=(
            P(("batch", "seq"), None),
            P("seq"),
            P("seq"),
            P(None, "mp"),
            P(None, "mp"),
            P(),
            P(None, "mp"),
            P(None, "mp"),
            P(),
            P("mp"),
            P("mp"),
            P("mp"),
            P("mp"),
        ),
        out_specs=P(("batch", "seq"), "mp"),
        check_vma=False,
    )
```

```python
import jax
import jax.numpy as jnp
from jax import lax
from jax.experimental import pallas as pl
from jax.experimental.pallas import tpu as pltpu
from jax.sharding import PartitionSpec as P

F32, BF, I32 = jnp.float32, jnp.bfloat16, jnp.int32
ROWS = 512
SEQ = 16
QUAD = ROWS // 4
SLOT = QUAD + 16
WIN = 32
KEYS = SEQ * WIN
CH = 64
BLOCK = 256
BC = 128
MIB = 1 << 20


def iota(shape, dim):
    return lax.broadcasted_iota(I32, shape, dim)


def dot(a, b, dims=((1,), (0,))):
    return lax.dot_general(a, b, (dims, ((), ())), preferred_element_type=F32)


def column(row):
    return jnp.transpose(jnp.broadcast_to(row, (128, row.shape[1])))


def tiles(row):
    return [row[:, g : g + 128] for g in range(0, row.shape[1], 128)]


def sorted_place(inv, inv_col):
    rank = jnp.concatenate(
        [jnp.sum((inv_col < part).astype(F32), axis=0, keepdims=True) for part in tiles(inv)],
        axis=1,
    )
    packed = jnp.floor(rank * 0.25)
    return (rank - 4.0 * packed) * QUAD + packed


def one_hot(place, count):
    row = iota((count, place.shape[1]), 0).astype(jnp.int16)
    return jnp.where(row == place.astype(I32).astype(jnp.int16), BF(1), BF(0))


def stacked(rows, shape):
    place = iota(shape, 0)
    block = jnp.zeros(shape, F32)
    for index, row in enumerate(rows):
        block = jnp.where(place == index, row, block)
    return block


def side_by_side(low, high):
    first = iota((QUAD, 128), 1) < 64
    return [
        jnp.where(first, low[u : u + QUAD], high[u + QUAD : u + 2 * QUAD]) for u in (0, 2 * QUAD)
    ]


def front_body(
    inv_hbm,
    ord_hbm,
    lat_hbm,
    wio_hbm,
    ws_ref,
    out_ref,
    inv_ref,
    ord_ref,
    lat_ref,
    wio_ref,
    sem_ref,
):
    small = [
        pltpu.make_async_copy(inv_hbm, inv_ref, sem_ref.at[0]),
        pltpu.make_async_copy(ord_hbm, ord_ref, sem_ref.at[1]),
    ]
    large = []
    for k in range(8):
        part = pl.ds(256 * k, 256)
        large.append(
            (
                pltpu.make_async_copy(lat_hbm.at[:, part], lat_ref.at[:, part], sem_ref.at[2 + k]),
                pltpu.make_async_copy(wio_hbm.at[part], wio_ref.at[part], sem_ref.at[10 + k]),
            )
        )
    for copy in small:
        copy.start()
    for pair in large:
        for copy in pair:
            copy.start()
    for copy in small:
        copy.wait()
    inv = inv_ref[...].astype(F32)
    inv_col = column(inv)
    deal = one_hot(sorted_place(inv, inv_col), ROWS)
    source = (ord_ref[...] >> 9).astype(F32)
    source_col = column(source)
    earlier = [
        jnp.sum(
            jnp.where(
                (source_col == part) & (iota((ROWS, 128), 0) < iota((ROWS, 128), 1) + 128 * g),
                1.0,
                0.0,
            ),
            axis=0,
            keepdims=True,
        )
        for g, part in enumerate(tiles(source))
    ]
    bound = (iota((ROWS, 128), 1) * ROWS).astype(F32)
    start = jnp.sum((inv_col < bound).astype(F32), axis=0, keepdims=True)
    tile = jnp.minimum(jnp.floor(start * (1.0 / 64.0)), 6.0)
    offset = start - 64.0 * tile
    blank = jnp.zeros((1, 128), F32)
    rows = [
        source[:, :256],
        source[:, 256:],
        jnp.concatenate(earlier[:2], axis=1),
        jnp.concatenate(earlier[2:], axis=1),
        jnp.concatenate([tile, blank], axis=1),
        jnp.concatenate([offset, blank], axis=1),
    ]
    io = jnp.zeros((ROWS, 256), F32)
    rest = jnp.zeros((ROWS, 128), F32)
    ws = jnp.concatenate([ws_ref[...], jnp.zeros((120, ws_ref.shape[1]), BF)], axis=0)
    for k, pair in enumerate(large):
        for copy in pair:
            copy.wait()
        part = slice(256 * k, 256 * k + 256)
        io = io + dot(lat_ref[:, part], wio_ref[part, :])
        rest = rest + dot(lat_ref[:, part], ws[:, part], ((1,), (1,)))
    io = dot(deal, io.astype(BF))
    rest = jnp.transpose(rest)[:8]
    pieces = []
    for _ in range(3):
        piece = rest.astype(BF)
        pieces.append(piece.astype(F32))
        rest = rest - pieces[-1]
    pieces = jnp.concatenate(pieces + [rest], axis=0).astype(BF)
    dealt = dot(pieces, deal, ((1,), (1,)))
    steps = [dealt[8 * k : 8 * k + 8] for k in range(3)]
    m = lax.axis_index("mp")
    half = jnp.where(m >= 2, io[:, 128:], io[:, :128])
    turned = pltpu.roll(half, 64, 1)
    odd = m % 2 == 1
    packed = side_by_side(jnp.where(odd, turned, half), jnp.where(odd, half, turned))
    slot = jnp.concatenate(packed, axis=1).astype(BF)
    for head in range(out_ref.shape[0]):
        halves = []
        for step in steps:
            own = step[head : head + 1]
            halves += [own[:, :256], own[:, 256:]]
        out_ref[head, :QUAD, :] = slot
        out_ref[head, QUAD:, :] = stacked(rows + halves, (16, 256)).astype(BF)


def value_body(inv_ref, lat_ref, wv_ref, out_ref, deal_ref):
    @pl.when(pl.program_id(0) == 0)
    def _():
        inv = inv_ref[...].astype(F32)
        deal_ref[...] = one_hot(sorted_place(inv, column(inv)), ROWS)

    value = dot(lat_ref[...], wv_ref[...]).astype(BF)
    value = dot(deal_ref[...], value)
    for jj in range(4):
        group = value[:, 128 * (jj // 2) : 128 * (jj // 2) + 128]
        turned = pltpu.roll(group, 64, 1)
        packed = side_by_side(group, turned) if jj % 2 == 0 else side_by_side(turned, group)
        out_ref[jj] = jnp.concatenate(packed, axis=1).astype(BF)


def silu(x):
    half = 0.5 * x
    return half + half * jnp.tanh(half)


def conv_silu(cur, prev, taps):
    ext = jnp.concatenate([prev, cur], axis=1)
    total = cur * taps[3]
    for back in range(1, 4):
        total = total + pltpu.roll(ext, back, 1)[:, 128:] * taps[3 - back]
    return silu(total)


def pick_quarter(res, quarter):
    out = jnp.zeros((CH, res.shape[1]), F32)
    for q in range(4):
        out = out + jnp.where(quarter == q, res[CH * q : CH * q + CH], 0.0)
    return out


def code_body(at_ref, ab_ref, own_ref, oth_ref, code_ref):
    c = at_ref[1]
    for z in range(8):
        for ref, core in ((own_ref, c), (oth_ref, 1 - c)):
            d = 2 * z + core
            side = ref[z, QUAD:SLOT, :].astype(F32)
            source = jnp.concatenate([side[0:1], side[1:2]], axis=1).astype(I32)
            place = jnp.concatenate([side[2:3], side[3:4]], axis=1).astype(I32)
            for s in range(SEQ):
                j = (s >> 1) + 8 * ((s + c) % 2)
                place = place + jnp.where(source == s, ab_ref[32 * j + 16 + d], 0)
            code_ref[pl.ds(d, 1), :] = source * 128 + place


def bc_body(
    at_ref, ab_ref, own_ref, oth_ref, conv_ref, out_a, out_b, code_ref, win_ref, tap_ref
):
    code_body(at_ref, ab_ref, own_ref, oth_ref, code_ref)
    m, c = at_ref[0], at_ref[1]
    group = conv_ref[:, pl.ds(pl.multiple_of(128 * (m // 2), 128), 128)]
    tap_ref[...] = jnp.transpose(stacked([group[k : k + 1] for k in range(4)], (128, 128)))
    tap_cols = tap_ref[pl.ds(pl.multiple_of(64 * (m % 2), 64), 64), :]
    taps = [tap_cols[:, k : k + 1] for k in range(4)]

    def rows_of(d, lo, hi):
        for j in range(SEQ):
            ref = own_ref if j < 8 else oth_ref
            at = pl.multiple_of(16 * ab_ref[32 * j + d], 16)
            win_ref[WIN * j : WIN * j + WIN, :] = ref[j % 8, pl.ds(at, WIN), :]
        code = code_ref[pl.ds(d, 1), :][:, lo:hi]
        source = code >> 7
        j_of = (source >> 1) + 8 * ((source + c) & 1)
        key = j_of * WIN + ((code >> 2) & (WIN - 1))
        spread = one_hot(key, KEYS)
        return pick_quarter(dot(win_ref[...], spread, ((0,), (0,))), code & 3)

    first = 8 * c
    prev = rows_of(jnp.maximum(first - 1, 0), ROWS - 128, ROWS)
    prev = jnp.where(first > 0, prev, 0.0)

    for e in range(8):
        cur = rows_of(first + e, 0, ROWS)
        out_ref = out_a if e < 4 else out_b
        out_ref[:, ROWS * (e % 4) : ROWS * (e % 4) + ROWS] = conv_silu(cur, prev, taps).astype(BF)
        prev = cur[:, ROWS - 128 :]


def tile_at(ab_ref, c, s, d):
    j = (s >> 1) + 8 * ((s + c) % 2)
    return pl.multiple_of(16 * ab_ref[32 * j + d], 16)


def time_body(
    at_ref, ab_ref, bias_ref, rate_ref, skip_ref, code_ref, own_ref, oth_ref, conv_ref,
    table_ref, win_ref, col_ref, step_ref, tap_ref
):
    c, sq = at_ref[1], at_ref[2]
    head = sq // 2
    group = conv_ref[:, pl.ds(pl.multiple_of(128 * head, 128), 128)]
    tap_ref[...] = jnp.transpose(stacked([group[k : k + 1] for k in range(4)], (128, 128)))
    table_ref[64:, :128] = tap_ref[pl.ds(pl.multiple_of(64 * (sq % 2), 64), 64), :]
    table_ref[0:SEQ, :] = code_ref[...].astype(F32)
    table_ref[48:64, :] = jnp.full((16, ROWS), skip_ref[head], F32)
    for core, ref in enumerate((own_ref, oth_ref)):
        blocks = []
        for z in range(8):
            side = ref[z, QUAD:SLOT, :].astype(F32)
            side = pltpu.roll(side, 10, 0)[0:8]
            blocks += [side[:, :128], side[:, 128:]]
        turned = jnp.transpose(jnp.concatenate(blocks, axis=0))
        for z in range(8):
            own = turned if z == 0 else pltpu.roll(turned, 128 - 16 * z, 1)
            col_ref[8 * core + z] = own.astype(BF)

    def gather(d, carry):
        for j in range(SEQ):
            at = pl.multiple_of(16 * ab_ref[32 * j + d], 16)
            win_ref[WIN * j : WIN * j + WIN, :] = col_ref[j, pl.ds(at, WIN), :]
        code = code_ref[pl.ds(d, 1), :]
        source = code >> 7
        j_of = (source >> 1) + 8 * ((source + c) & 1)
        spread = one_hot(j_of * WIN + ((code >> 2) & (WIN - 1)), KEYS)
        quarter = code & 3
        parts = dot(win_ref[...], spread, ((0,), (0,)))
        step = jnp.zeros((1, ROWS), F32)
        for q in range(4):
            row = (q >> 1) + 8 * (q & 1)
            value = parts[row : row + 1] + parts[row + 2 : row + 3] + parts[row + 4 : row + 5]
            step = step + jnp.where(quarter == q, value, 0.0)
        step_ref[pl.ds(d, 1), :] = step
        return carry

    lax.fori_loop(0, SEQ, gather, 0, unroll=4)

    raw = step_ref[...] + bias_ref[head]
    size = jnp.maximum(raw, 0.0) + jnp.log1p(jnp.exp(-jnp.abs(raw)))
    table_ref[SEQ : 2 * SEQ, :] = size
    rate = jnp.exp(jnp.full((1, ROWS), rate_ref[head], F32))
    cum = -rate * size
    lane = iota((SEQ, ROWS), 1) & (BLOCK - 1)
    shift = 1
    while shift < BLOCK:
        cum = cum + jnp.where(lane >= shift, pltpu.roll(cum, shift, 1), 0.0)
        shift *= 2
    table_ref[2 * SEQ : 3 * SEQ, :] = cum


def gate_body(lat_ref, w_ref, out_ref):
    out_ref[...] = silu(dot(lat_ref[...], w_ref[...])).astype(BF)


def spread_of(table_ref, d):
    code = table_ref[pl.ds(d, 1), :].astype(I32)
    return one_hot((code >> 7) * WIN + ((code >> 2) & (WIN - 1)), KEYS), code & 3


def place_half(first, prev, at_ref, ab_ref, table_ref, x_ref, xact_ref, win_ref):
    c = at_ref[1]
    taps = [table_ref[64:, k : k + 1] for k in range(4)]

    def gather(e, prev):
        d = first + e
        for s in range(SEQ):
            at = tile_at(ab_ref, c, s, d)
            win_ref[WIN * s : WIN * s + WIN, :] = x_ref[s, pl.ds(at, WIN), :]
        spread, quarter = spread_of(table_ref, d)
        cur = pick_quarter(dot(win_ref[...], spread, ((0,), (0,))), quarter)
        act = conv_silu(cur, prev, taps)
        xact_ref[:, pl.ds(pl.multiple_of(ROWS * e, ROWS), ROWS)] = act.astype(BF)
        return cur[:, ROWS - 128 :]

    return lax.fori_loop(0, SEQ // 2, gather, prev, unroll=8)


def place_first(at_ref, ab_ref, table_ref, x_ref, *refs):
    parts, (xact_ref, last_ref, bundle_ref, win_ref, sem_ref) = refs[:4], refs[4:]
    copies = [
        pltpu.make_async_copy(part, bundle_ref.at[k], sem_ref.at[k]) for k, part in enumerate(parts)
    ]
    for copy in copies:
        copy.start()
    prev = jnp.zeros((CH, 128), F32)
    last_ref[...] = place_half(0, prev, at_ref, ab_ref, table_ref, x_ref, xact_ref, win_ref)
    for copy in copies:
        copy.wait()


def place_second(at_ref, ab_ref, table_ref, x_ref, last_ref, xact_ref, win_ref):
    place_half(8, last_ref[...], at_ref, ab_ref, table_ref, x_ref, xact_ref, win_ref)


def scan_body(at_ref, ab_ref, table_ref, xact_a, xact_b, *refs):
    owns, bundle, late = refs[:8], refs[8], refs[9:13]
    out_ref, bc_ref, sem_ref = refs[13:]
    oths = [bundle.at[0], bundle.at[1], bundle.at[2], *late, bundle.at[3]]
    m, c = at_ref[0], at_ref[1]
    copies = []
    for index in range(8):
        rows = pl.ds(pl.multiple_of(CH * ((m - index // 2 + 4) % 4), CH), CH)
        cols = pl.ds(4 * ROWS * (index % 2), 4 * ROWS)
        for side, ref in enumerate((owns[index], oths[index])):
            half = c if side == 0 else 1 - c
            copies.append(
                pltpu.make_async_copy(ref, bc_ref.at[half, rows, cols], sem_ref.at[index, side])
            )
    for copy in copies:
        copy.start()
    out_ref[...] = jnp.zeros_like(out_ref)
    skip = table_ref[48:49, :BLOCK]
    causal = iota((BLOCK, BLOCK), 0) <= iota((BLOCK, BLOCK), 1)
    def scan(half, e, state):
        d = 8 * half + e
        cols = pl.ds(pl.multiple_of(ROWS * e, ROWS), ROWS)
        x_all = (xact_b if half else xact_a)[:, cols].astype(F32)
        bc = bc_ref[half, :, cols]
        size_all = table_ref[pl.ds(SEQ + d, 1), :]
        cum_all = table_ref[pl.ds(2 * SEQ + d, 1), :]
        ys = []
        for k in range(ROWS // BLOCK):
            at = slice(BLOCK * k, BLOCK * k + BLOCK)
            x, b, cc = x_all[:, at], bc[:BC, at], bc[BC:, at]
            cum_row, size = cum_all[:, at], size_all[:, at]
            scores = dot(b, cc, ((0,), (0,)))
            col = column(cum_row)
            gap = cum_row - jnp.concatenate([col] * (BLOCK // 128), axis=1)
            weight = (scores * jnp.exp(jnp.where(causal, gap, -1e30))).astype(BF)
            y = dot((x * size).astype(BF), weight)
            y = y + dot(state.astype(BF), cc) * jnp.exp(cum_row) + skip * x
            ys.append(y)
            total = cum_row[:, BLOCK - 1 :]
            scaled = (x * (jnp.exp(total - cum_row) * size)).astype(BF)
            state = jnp.exp(total) * state + dot(scaled, b, ((1,), (1,)))
        y_all = jnp.concatenate(ys, axis=1)
        spread, quarter = spread_of(table_ref, d)
        apart = jnp.concatenate(
            [jnp.where(quarter == q, y_all, 0.0).astype(BF) for q in range(4)], axis=0
        )
        back = dot(spread, apart, ((1,), (1,)))
        for s in range(SEQ):
            at = pl.ds(tile_at(ab_ref, c, s, d), WIN)
            out_ref[s, at, :] = out_ref[s, at, :] + back[WIN * s : WIN * s + WIN].astype(BF)
        return state

    state = jnp.zeros((CH, BC), F32)
    for half in range(2):
        for index in range(8):
            rows = pl.ds(pl.multiple_of(CH * ((m - index // 2 + 4) % 4), CH), CH)
            cols = pl.ds(4 * ROWS * (index % 2), 4 * ROWS)
            sem = sem_ref.at[index, c if half == 0 else 1 - c]
            pltpu.make_async_copy(owns[index], bc_ref.at[half, rows, cols], sem).wait()
        state = lax.fori_loop(0, 8, lambda e, state, half=half: scan(half, e, state), state, unroll=8)


def final_body(inv_ref, y_ref, gate_hbm, gain_ref, out_ref, pick_ref, gate_ref, sem_ref):
    h = pl.program_id(0)

    def gate_copy(n):
        part = pl.ds(pl.multiple_of(512 * n, 512), 512)
        return pltpu.make_async_copy(gate_hbm.at[:, part], gate_ref.at[n], sem_ref.at[n])

    @pl.when(h == 0)
    def _():
        for n in range(gate_ref.shape[0]):
            gate_copy(n).start()
        inv = inv_ref[...].astype(F32)
        place = column(sorted_place(inv, column(inv)))
        lane = iota((ROWS, 128), 1)
        for g in range(4):
            hit = place == (lane + 128 * g).astype(F32)
            pick_ref[:, 128 * g : 128 * g + 128] = hit.astype(F32).astype(BF)

    low = iota((QUAD, 128), 1) < 64
    heads = []
    for n in range(4):
        rows = []
        for q in range(4):
            at = slice(128 * (q // 2), 128 * (q // 2) + 128)
            even = y_ref[8 * h + 2 * n, :, at].astype(F32)
            odd = y_ref[8 * h + 2 * n + 1, :, at].astype(F32)
            if q % 2 == 0:
                rows.append(jnp.where(low, even, pltpu.roll(odd, 64, 1)))
            else:
                rows.append(jnp.where(low, pltpu.roll(even, 64, 1), odd))
        heads.append(jnp.concatenate(rows, axis=0).astype(BF))
    y = dot(pick_ref[...], jnp.concatenate(heads, axis=1))
    gate_copy(h).wait()
    for n in range(4):
        at = slice(128 * n, 128 * n + 128)
        gated = y[:, at] * gate_ref[h, :, at].astype(F32)
        mean = jnp.mean(gated * gated, axis=1, keepdims=True)
        out_ref[:, at] = (gated * lax.rsqrt(mean + 1e-5) * gain_ref[:, at]).astype(BF)


def vmem(*_):
    return pl.BlockSpec(memory_space=pltpu.VMEM)


def hbm(*_):
    return pl.BlockSpec(memory_space=pl.ANY)


def smem(*_):
    return pl.BlockSpec(memory_space=pltpu.SMEM)


def params(mib):
    return pltpu.CompilerParams(vmem_limit_bytes=mib * MIB)


def cost(flops, data, exps=0):
    return pl.CostEstimate(flops=flops, bytes_accessed=data, transcendentals=exps)


def run_time(*args):
    return pl.pallas_call(
        time_body,
        out_shape=jax.ShapeDtypeStruct((128, ROWS), F32),
        in_specs=[smem()] * 5 + [vmem()] * 4,
        out_specs=vmem(),
        scratch_shapes=[
            pltpu.VMEM((KEYS, 128), BF),
            pltpu.VMEM((SEQ, 128, 128), BF),
            pltpu.VMEM((SEQ, ROWS), F32),
            pltpu.VMEM((128, 128), F32),
        ],
        compiler_params=params(8),
        cost_estimate=cost(2 << 30, 2 << 20),
        name="time",
    )(*args)


def run_place(kernel, outs, args, parts=()):
    sems = [pltpu.SemaphoreType.DMA((len(parts),))] if parts else []
    return pl.pallas_call(
        kernel,
        out_shape=outs,
        in_specs=[smem()] * 2 + [vmem()] * (len(args) - 2) + [hbm()] * len(parts),
        out_specs=tuple(vmem() for _ in outs),
        scratch_shapes=[pltpu.VMEM((KEYS, 256), BF), *sems],
        compiler_params=params(24),
        cost_estimate=cost(2 << 30, 2 << 20),
        name="place",
    )(*args, *parts)


def run_scan(*args):
    return pl.pallas_call(
        scan_body,
        out_shape=jax.ShapeDtypeStruct((SEQ, QUAD, 256), BF),
        in_specs=[smem()] * 2 + [vmem()] * 3 + [hbm()] * 13,
        out_specs=vmem(),
        scratch_shapes=[
            pltpu.VMEM((2, 256, 8 * ROWS), BF),
            pltpu.SemaphoreType.DMA((8, 2)),
        ],
        compiler_params=params(24),
        cost_estimate=cost(8 << 30, 8 << 20),
        name="scan",
    )(*args)


def run_front(*args):
    return pl.pallas_call(
        front_body,
        out_shape=jax.ShapeDtypeStruct((8, SLOT, 256), BF),
        in_specs=[hbm(), hbm(), hbm(), hbm(), vmem()],
        out_specs=vmem(),
        scratch_shapes=[
            pltpu.VMEM((1, ROWS), I32),
            pltpu.VMEM((1, ROWS), I32),
            pltpu.VMEM(args[2].shape, BF),
            pltpu.VMEM(args[3].shape, BF),
            pltpu.SemaphoreType.DMA((18,)),
        ],
        compiler_params=params(60),
        cost_estimate=cost(1 << 30, 4 << 20),
        name="front",
    )(*args)


def run_final(*args):
    heads = args[1].shape[0] // 2
    return pl.pallas_call(
        final_body,
        grid=(heads // 4,),
        out_shape=jax.ShapeDtypeStruct((ROWS, heads * 128), BF),
        in_specs=[
            pl.BlockSpec((1, ROWS), lambda h: (0, 0)),
            vmem(),
            hbm(),
            pl.BlockSpec((1, 512), lambda h: (0, h)),
        ],
        out_specs=pl.BlockSpec((ROWS, 512), lambda h: (0, h)),
        scratch_shapes=[
            pltpu.VMEM((ROWS, ROWS), BF),
            pltpu.VMEM((heads // 4, ROWS, 512), BF),
            pltpu.SemaphoreType.DMA((heads // 4,)),
        ],
        compiler_params=params(12),
        cost_estimate=cost(1 << 30, 3 << 20),
        name="final",
    )(*args)


def body(
    latent,
    order,
    inverse,
    w_gate,
    w_value,
    w_input_output,
    w_step,
    conv_value,
    conv_input_output,
    step_bias,
    log_rate,
    skip_gain,
    norm_gain,
):
    m, sq = lax.axis_index("mp"), lax.axis_index("seq")
    at = jnp.stack([m, sq % 2, sq, m]).astype(I32)
    inv = inverse.reshape(1, ROWS)
    pairs = [(i, i ^ 1) for i in range(SEQ)]
    lines = [[2 * i + core for i in range(SEQ // 2)] for core in range(2)]

    bc_slots = run_front(inv, order.reshape(1, ROWS), latent, w_input_output, w_step.T)
    own = lax.all_to_all(bc_slots, "seq", 0, 0, axis_index_groups=lines, tiled=True)

    x_slots = pl.pallas_call(
        value_body,
        grid=(4,),
        out_shape=jax.ShapeDtypeStruct((SEQ, QUAD, 256), BF),
        in_specs=[
            pl.BlockSpec((1, ROWS), lambda n: (0, 0)),
            pl.BlockSpec((ROWS, latent.shape[1]), lambda n: (0, 0)),
            pl.BlockSpec((latent.shape[1], 256), lambda n: (0, n)),
        ],
        out_specs=pl.BlockSpec((4, QUAD, 256), lambda n: (n, 0, 0)),
        scratch_shapes=[pltpu.VMEM((ROWS, ROWS), BF)],
        compiler_params=params(24),
        cost_estimate=cost(3 << 30, 8 << 20),
        name="value",
    )(inv, latent, w_value)
    gate = pl.pallas_call(
        gate_body,
        grid=(4,),
        out_shape=jax.ShapeDtypeStruct((ROWS, w_gate.shape[1]), BF),
        in_specs=[
            pl.BlockSpec((ROWS, latent.shape[1]), lambda n: (0, 0)),
            pl.BlockSpec((latent.shape[1], 256), lambda n: (0, n)),
        ],
        out_specs=pl.BlockSpec((ROWS, 256), lambda n: (0, n)),
        compiler_params=params(24),
        cost_estimate=cost(2 << 30, 8 << 20),
        name="gate",
    )(latent, w_gate)

    x_slots, own = lax.optimization_barrier((x_slots, own))
    oth = lax.ppermute(own, "seq", pairs)
    x_all = lax.all_to_all(x_slots, "seq", 0, 0, tiled=True)

    side = jnp.concatenate([own[:, QUAD + 4 : QUAD + 6, :16], oth[:, QUAD + 4 : QUAD + 6, :16]], 0)
    ab = side.astype(I32).reshape(-1)
    half = jax.ShapeDtypeStruct((CH, 4 * ROWS), BF)
    bc_a, bc_b, code = pl.pallas_call(
        bc_body,
        out_shape=(half, half, jax.ShapeDtypeStruct((SEQ, ROWS), I32)),
        in_specs=[smem(), smem(), vmem(), vmem(), vmem()],
        out_specs=(vmem(), vmem(), vmem()),
        scratch_shapes=[pltpu.VMEM((KEYS, 256), BF), pltpu.VMEM((128, 128), F32)],
        compiler_params=params(8),
        cost_estimate=cost(1 << 30, 2 << 20),
        name="bc",
    )(at, ab, own, oth, conv_input_output)
    up = [(i, (i + 1) % 4) for i in range(4)]
    down = [(i, (i - 1) % 4) for i in range(4)]
    one_a, three_b = lax.ppermute(bc_a, "mp", up), lax.ppermute(bc_b, "mp", down)
    one_b, three_a = lax.ppermute(bc_b, "mp", up), lax.ppermute(bc_a, "mp", down)
    table = run_time(at, ab, step_bias, log_rate, skip_gain, code, own, oth, conv_value)
    one_a, three_b, table = lax.optimization_barrier((one_a, three_b, table))
    two_a, two_b = lax.ppermute(one_a, "mp", up), lax.ppermute(three_b, "mp", down)
    owns = [bc_a, bc_b, one_a, one_b, two_a, two_b, three_a, three_b]
    part = jax.ShapeDtypeStruct((CH, 8 * ROWS), BF)
    last = jax.ShapeDtypeStruct((CH, 128), F32)
    sheaf = jax.ShapeDtypeStruct((4, CH, 4 * ROWS), BF)
    xact_a, last, bundle = run_place(
        place_first, (part, last, sheaf), (at, ab, table, x_all), (bc_a, bc_b, one_a, three_b)
    )
    late, bundle, xact_a = lax.optimization_barrier((owns[3:7], bundle, xact_a))
    owns = [*owns[:3], *late, owns[7]]
    oths = [lax.ppermute(v, "seq", pairs) for v in (bundle, *late)]
    (xact_b,) = run_place(place_second, (part,), (at, ab, table, x_all, last))
    y_slots = run_scan(at, ab, table, xact_a, xact_b, *owns, *oths)
    y_all = lax.all_to_all(y_slots, "seq", 0, 0, tiled=True)

    return run_final(inv, y_all, gate, norm_gain.reshape(1, -1))


def solution(mesh):
    return jax.shard_map(
        body,
        mesh=mesh,
        in_specs=(
            P(("batch", "seq"), None),
            P("seq"),
            P("seq"),
            P(None, "mp"),
            P(None, "mp"),
            P(),
            P(None, "mp"),
            P(None, "mp"),
            P(),
            P("mp"),
            P("mp"),
            P("mp"),
            P("mp"),
        ),
        out_specs=P(("batch", "seq"), "mp"),
        check_vma=False,
    )
```
